32 devices in a mesh: row: 4 (over x, core), col: 8 (over z, y).
Axes of the slice: x: 2, y: 2, z: 4, core: 2. Of those that a mesh axis runs over, the one named last changes fastest.
Arguments:
- contact: bfloat16 [256, 16384], P('row', 'col'), may hold values from -6 to 6
- first_down: bfloat16 [2, 3, 3, 32, 64], replicated, may hold values from -0.25 to 0.25
- first_down_bias: float32 [2, 32], replicated, may hold values from -1.5 to 1.5
- first_up: bfloat16 [2, 3, 3, 64, 32], replicated, may hold values from -0.375 to 0.375
- first_up_bias: float32 [2, 64], replicated, may hold values from -1.5 to 1.5
- second_down: bfloat16 [2, 3, 3, 32, 64], replicated, may hold values from -0.25 to 0.25
- second_down_bias: float32 [2, 32], replicated, may hold values from -1.5 to 1.5
- second_up: bfloat16 [2, 3, 3, 64, 32], replicated, may hold values from -0.375 to 0.375
- second_up_bias: float32 [2, 64], replicated, may hold values from -1.5 to 1.5
Outputs:
- decoded: bfloat16 [256, 16384], P('row', 'col')
The draws below stay inside these ranges and needn't reach their ends.
All inputs are finite; a program needn't handle non-finite values.
Results may differ from the reference program's by a relative error of at most 0.012.
Values may be sent and summed in bfloat16 or wider, within the bound.
A program may use at most 64 MiB of HBM per device.

```python
import jax
import jax.numpy as jnp
from jax import lax

C = 64
CI = 32
H = 256
W = 256


def shard_levels(key, dims, pieces, low, high):
    gain, own = 1.0, jax.random.fold_in(key, 6)
    for axis_at, shards_of in pieces:
        heights = jnp.exp(jax.random.uniform(jax.random.fold_in(own, axis_at), (shards_of,), jnp.float32, low / len(pieces), high / len(pieces)))
        gain = gain * jnp.repeat(heights, dims[axis_at] // shards_of).reshape([-1 if axis == axis_at else 1 for axis in range(len(dims))])
    return gain


def normal_values(key, dims, scale, reach, shards=(), held_as=jnp.bfloat16):
    values = jax.random.normal(key, dims, jnp.float32) * scale
    if len(shards) > 0:
        values = shard_levels(key, dims, shards, -0.22, 0.18) * values
    return jnp.clip(values, min=-reach, max=reach).astype(held_as)


def setup_inputs(seed: int = 0) -> dict:
    splits = jax.random.split(jax.random.key(seed), 10)
    contact = normal_values(splits[0], (H, W * C), 1.0, 6.0, ((0, 4), (1, 8)))
    first_down = normal_values(splits[1], (2, 3, 3, CI, C), (9 * C) ** -0.5, 0.25)
    first_down_bias = normal_values(splits[2], (2, CI), 0.3, 1.5, (), jnp.float32)
    first_up = normal_values(splits[3], (2, 3, 3, C, CI), (9 * CI) ** -0.5, 0.375)
    first_up_bias = normal_values(splits[4], (2, C), 0.3, 1.5, (), jnp.float32)
    second_down = normal_values(splits[5], (2, 3, 3, CI, C), (9 * C) ** -0.5, 0.25)
    second_down_bias = normal_values(splits[6], (2, CI), 0.3, 1.5, (), jnp.float32)
    second_up = normal_values(splits[7], (2, 3, 3, C, CI), (9 * CI) ** -0.5, 0.375)
    second_up_bias = normal_values(splits[8], (2, C), 0.3, 1.5, (), jnp.float32)
    return {"contact": contact, "first_down": first_down, "first_down_bias": first_down_bias, "first_up": first_up, "first_up_bias": first_up_bias, "second_down": second_down, "second_down_bias": second_down_bias, "second_up": second_up, "second_up_bias": second_up_bias}


def convolve(field, weight, bias_term, dilation):
    result = lax.conv_general_dilated(
        field.astype(jnp.float32)[None],
        weight.astype(jnp.float32).transpose(2, 3, 0, 1),
        (1, 1),
        [(dilation, dilation), (dilation, dilation)],
        rhs_dilation=(dilation, dilation),
        dimension_numbers=("NCHW", "OIHW", "NCHW"),
        precision=lax.Precision.HIGHEST,
    )[0]
    return result + bias_term[:, None, None]


def run_section(field, down_weight, down_bias, up_weight, up_bias):
    for block_index, dilations in enumerate(((1, 2), (4, 8))):
        hidden = jax.nn.relu(convolve(field, down_weight[block_index], down_bias[block_index], dilations[0])).astype(jnp.bfloat16)
        update = convolve(hidden, up_weight[block_index], up_bias[block_index], dilations[1])
        field = (field.astype(jnp.float32) + update).astype(jnp.bfloat16)
    return field


def reference(contact, first_down, first_down_bias, first_up, first_up_bias, second_down, second_down_bias, second_up, second_up_bias):
    field = contact.reshape(H, W, C).transpose(2, 0, 1)
    first = run_section(field, first_down, first_down_bias, first_up, first_up_bias)
    widened = first.astype(jnp.float32)
    symmetric = ((widened + widened.transpose(0, 2, 1)) * 0.5).astype(jnp.bfloat16)
    result = run_section(symmetric, second_down, second_down_bias, second_up, second_up_bias)
    return result.transpose(1, 2, 0).reshape(H, W * C)
```

```python
import functools

import jax
import jax.numpy as jnp
from jax import lax
from jax.experimental import pallas as pl
from jax.experimental.pallas import tpu as pltpu
from jax.sharding import PartitionSpec as P

MESH = pl.DeviceIdType.MESH
HALO = 16
SIDE = HALO // 2
BLOCKS = ((1, 2), (4, 8))
WAYS = ((0, -1), (0, 1), (-1, 0), (1, 0), (-1, -1), (-1, 1), (1, -1), (1, 1))
NT = (((1,), (1,)), ((), ()))


def chunk_of(count, most):
    return max(n for n in range(1, most + 1) if count % n == 0)


def kernel(
    rows_of, cols_of,
    contact, fd, fdb, fu, fub, sd, sdb, su, sub,
    out,
    v1, v2, hid, mirror, wide, flipped, wd, wu, bias,
    send1, recv1, send2, recv2, send_m, recv_m, local_sem,
):
    tile_rows = contact.shape[0]
    pairs = contact.shape[1] // 128
    span = tile_rows + 2 * HALO
    all_pairs = pairs + 2 * SIDE
    square = 2 * pairs
    fold = tile_rows // square
    r = lax.axis_index("row")
    c = lax.axis_index("col")
    up_edge, down_edge = r == 0, r == rows_of - 1
    left_edge, right_edge = c == 0, c == cols_of - 1

    def there(dr, dc):
        return (r + dr >= 0) & (r + dr < rows_of) & (c + dc >= 0) & (c + dc < cols_of)

    mirror_row = lax.div(c, fold)
    peers = [(mirror_row, fold * r + m) for m in range(fold)]
    slot = lax.rem(c, fold)

    def is_me(peer):
        return (peer[0] == r) & (peer[1] == c)

    barrier = pltpu.get_barrier_semaphore()
    greeted = jnp.int32(0)
    for dr, dc in WAYS:
        ok = there(dr, dc)
        greeted += ok.astype(jnp.int32)

        @pl.when(ok)
        def _():
            pl.semaphore_signal(barrier, inc=1, device_id=(r + dr, c + dc), device_id_type=MESH)

    for peer in peers:
        other = jnp.logical_not(is_me(peer))
        greeted += other.astype(jnp.int32)

        @pl.when(other)
        def _():
            pl.semaphore_signal(barrier, inc=1, device_id=peer, device_id_type=MESH)

    def clear(buf, first, last, lanes=slice(None)):
        rows = buf.shape[1]
        width = 128 if lanes == slice(None) else 64
        buf[first:last, :, lanes] = jnp.zeros((last - first, rows, width), buf.dtype)

    def clear_rows(buf):
        strip = jnp.zeros((all_pairs, HALO, 128), buf.dtype)

        @pl.when(up_edge)
        def _():
            buf[:, 0:HALO, :] = strip

        @pl.when(down_edge)
        def _():
            buf[:, HALO + tile_rows : span, :] = strip

    def clear_outside(buf):
        clear_rows(buf)

        @pl.when(left_edge)
        def _():
            clear(buf, 0, SIDE)

        @pl.when(right_edge)
        def _():
            clear(buf, SIDE + pairs, all_pairs)

    def clear_hidden(s):
        clear_rows(hid)

        @pl.when(left_edge)
        def _():
            clear(hid, 0, SIDE, slice(0, 64))
            clear(hid, 0, SIDE - s, slice(64, 128))

        @pl.when(right_edge)
        def _():
            clear(hid, SIDE + pairs, all_pairs, slice(0, 64))
            clear(hid, SIDE + pairs - s, all_pairs, slice(64, 128))

    def halo_copies(buf, send, recv):
        copies = []
        for at, (dr, dc) in enumerate(WAYS):
            src_row = {-1: (HALO, HALO), 0: (HALO, tile_rows), 1: (tile_rows, HALO)}[dr]
            dst_row = {-1: HALO + tile_rows, 0: HALO, 1: 0}[dr]
            src_col = {-1: (SIDE, SIDE), 0: (SIDE, pairs), 1: (pairs, SIDE)}[dc]
            dst_col = {-1: SIDE + pairs, 0: SIDE, 1: 0}[dc]
            copies.append(
                pltpu.make_async_remote_copy(
                    src_ref=buf.at[pl.ds(*src_col), pl.ds(*src_row), :],
                    dst_ref=buf.at[pl.ds(dst_col, src_col[1]), pl.ds(dst_row, src_row[1]), :],
                    send_sem=send.at[at],
                    recv_sem=recv.at[at],
                    device_id=(jnp.clip(r + dr, 0, rows_of - 1), jnp.clip(c + dc, 0, cols_of - 1)),
                    device_id_type=MESH,
                )
            )
        return copies

    def start_halo(copies):
        for (dr, dc), copy in zip(WAYS, copies):
            pl.when(there(dr, dc))(copy.start)

    def finish_halo(copies):
        for (dr, dc), copy in zip(WAYS, copies):
            pl.when(there(-dr, -dc))(copy.wait_recv)
        for (dr, dc), copy in zip(WAYS, copies):
            pl.when(there(dr, dc))(copy.wait_send)

    def down(buf, at, d, s, s_up, low, high):
        n = chunk_of(high - low, 8)

        def step(i, carry):
            j = low + i * n
            x = jnp.concatenate(
                [buf[pl.ds(j - s, n)], buf[pl.ds(j, n)], buf[pl.ds(j + s, n)]], axis=-1
            ).reshape(n * span, 384)
            sums = lax.dot_general(x, wd[at], NT, preferred_element_type=jnp.float32)
            outer, middle = sums[:, :128], sums[:, 128:]
            h = pltpu.roll(outer, d, 0) + middle
            h = h + pltpu.roll(pltpu.roll(outer, 64, 1), n * span - d, 0)
            h = jnp.maximum(h + bias[at : at + 1, :], 0.0)
            moved = pltpu.roll(h, 64, 1)
            hid[pl.ds(j, n), :, 0:64] = h.astype(jnp.bfloat16).reshape(n, span, 128)[:, :, 0:64]
            hid[pl.ds(j - s_up, n), :, 64:128] = moved.astype(jnp.bfloat16).reshape(n, span, 128)[
                :, :, 64:128
            ]
            return carry

        lax.fori_loop(0, (high - low) // n, step, 0)

    def up(buf, at, d, s, low, high, store):
        n = chunk_of(high - low, 8)

        def step(i, carry):
            j = low + i * n
            x = jnp.concatenate([hid[pl.ds(j - s, n)], hid[pl.ds(j + s, n)]], axis=-1)
            sums = lax.dot_general(
                x.reshape(n * span, 256), wu[at], NT, preferred_element_type=jnp.float32
            )
            u = pltpu.roll(sums[:, :128], d, 0) + sums[:, 128:256]
            u = u + pltpu.roll(sums[:, 256:], n * span - d, 0)
            u = (u + bias[4 + at : 5 + at, :]).reshape(n, span, 128)
            store(j, n, u)
            return carry

        lax.fori_loop(0, (high - low) // n, step, 0)

    def section(buf, first_at, store_last):
        margin = 2 * SIDE
        used = 0
        for block, (d1, d2) in enumerate(BLOCKS):
            at = first_at + block
            s1, s2 = max(d1 // 2, 1), d2 // 2
            used += s1
            down(buf, at, d1, s1, s2, used, all_pairs - used)
            clear_hidden(s2)
            used += s2
            last = block == len(BLOCKS) - 1

            def store(j, n, u):
                v = buf[pl.ds(j, n)].astype(jnp.float32) + u
                buf[pl.ds(j, n)] = v.astype(jnp.bfloat16)

            up(buf, at, d2, s2, used, all_pairs - used, store_last if last else store)
            if not last:
                clear_outside(buf)

    for j in range(pairs):
        v1[SIDE + j, HALO : HALO + tile_rows, :] = contact[:, 128 * j : 128 * (j + 1)]
    pl.semaphore_wait(barrier, greeted)
    first_halo = halo_copies(v1, send1, recv1)
    start_halo(first_halo)

    clear_outside(v1)
    clear_outside(v2)
    hid[...] = jnp.zeros(hid.shape, hid.dtype)
    wd[...] = jnp.zeros(wd.shape, wd.dtype)
    wu[...] = jnp.zeros(wu.shape, wu.dtype)
    bias[...] = jnp.zeros(bias.shape, bias.dtype)
    for sec, (dw, db, uw, ub) in enumerate(((fd, fdb, fu, fub), (sd, sdb, su, sub))):
        for block, (d1, d2) in enumerate(BLOCKS):
            at = 2 * sec + block
            bias[at : at + 1, 0:32] = db[block : block + 1, :]
            bias[at : at + 1, 32:64] = db[block : block + 1, :]
            bias[4 + at : 5 + at, 0:64] = ub[block : block + 1, :]
            bias[4 + at : 5 + at, 64:128] = ub[block : block + 1, :]
            for p in range(3):
                group = (0, 128, 64)[p]
                for q in range(3):
                    for par in range(2):
                        shift = par + (q - 1) * d1
                        third = 1 + (shift // 2 > 0) - (shift // 2 < 0)
                        lane = third * 128 + (shift % 2) * 64
                        row = group + par * 32
                        wd[at, row : row + 32, lane : lane + 64] = dw[block, p, q]
                        row = p * 128 + par * 64
                        lane = q * 64 + par * 32
                        wu[at, row : row + 64, lane : lane + 32] = uw[block, p, q]

    finish_halo(first_halo)

    def store_first(j, n, u):
        inner = slice(HALO, HALO + tile_rows)
        v = v1[pl.ds(j, n), inner, :].astype(jnp.float32) + u[:, inner, :]
        v1[pl.ds(j, n), inner, :] = v.astype(jnp.bfloat16)

    section(v1, 0, store_first)

    mirrors = []
    for m, peer in enumerate(peers):
        src = v1.at[pl.ds(SIDE, pairs), pl.ds(HALO + m * square, square), :]
        remote = pltpu.make_async_remote_copy(
            src_ref=src,
            dst_ref=mirror.at[slot],
            send_sem=send_m.at[m],
            recv_sem=recv_m.at[slot],
            device_id=peer,
            device_id_type=MESH,
        )
        here = pltpu.make_async_copy(src, mirror.at[slot], local_sem)
        mirrors.append((peer, remote, here))
        pl.when(jnp.logical_not(is_me(peer)))(remote.start)
        pl.when(is_me(peer))(here.start)
    for m, (peer, remote, here) in enumerate(mirrors):
        arrived = pltpu.make_async_remote_copy(
            src_ref=mirror.at[m],
            dst_ref=mirror.at[m],
            send_sem=send_m.at[m],
            recv_sem=recv_m.at[m],
            device_id=peer,
            device_id_type=MESH,
        )
        pl.when(jnp.logical_not(is_me(peer)))(arrived.wait_recv)
        pl.when(is_me(peer))(here.wait)
    low_half = lax.broadcasted_iota(jnp.int32, (pairs, 128), 1) < 64
    for m in range(fold):
        wide[...] = mirror[m].astype(jnp.float32).reshape(pairs * square, 128)
        for j in range(pairs):
            even = wide[pl.ds(2 * j, pairs, stride=square), :]
            odd = wide[pl.ds(2 * j + 1, pairs, stride=square), :]
            base = j * tile_rows + m * square
            flipped[pl.ds(base, pairs, stride=2), :] = jnp.where(
                low_half, even, pltpu.roll(odd, 64, 1)
            )
            flipped[pl.ds(base + 1, pairs, stride=2), :] = jnp.where(
                low_half, pltpu.roll(even, 64, 1), odd
            )
    own = v1[SIDE : SIDE + pairs, HALO : HALO + tile_rows, :].astype(jnp.float32)
    both = (own + flipped[...].reshape(pairs, tile_rows, 128)) * 0.5
    v2[SIDE : SIDE + pairs, HALO : HALO + tile_rows, :] = both.astype(jnp.bfloat16)

    second_halo = halo_copies(v2, send2, recv2)
    start_halo(second_halo)
    for peer, remote, here in mirrors:
        pl.when(jnp.logical_not(is_me(peer)))(remote.wait_send)
    finish_halo(second_halo)

    def store_second(j, n, u):
        inner = slice(HALO, HALO + tile_rows)
        v = (v2[pl.ds(j, n), inner, :].astype(jnp.float32) + u[:, inner, :]).astype(jnp.bfloat16)
        for k in range(n):
            out[:, pl.ds(pl.multiple_of((j - SIDE + k) * 128, 128), 128)] = v[k]

    section(v2, 2, store_second)


def per_device(rows_of, cols_of, contact, *weights):
    tile_rows = contact.shape[0]
    pairs = contact.shape[1] // 128
    span, all_pairs, square = tile_rows + 2 * HALO, pairs + 2 * SIDE, 2 * pairs
    fold = tile_rows // square
    buf = pltpu.VMEM((all_pairs, span, 128), jnp.bfloat16)
    return pl.pallas_call(
        functools.partial(kernel, rows_of, cols_of),
        out_shape=jax.ShapeDtypeStruct(contact.shape, jnp.bfloat16),
        in_specs=[pl.BlockSpec(memory_space=pltpu.VMEM)] * (1 + len(weights)),
        out_specs=pl.BlockSpec(memory_space=pltpu.VMEM),
        scratch_shapes=[
            buf,
            buf,
            buf,
            pltpu.VMEM((fold, pairs, square, 128), jnp.bfloat16),
            pltpu.VMEM((pairs * square, 128), jnp.float32),
            pltpu.VMEM((pairs * tile_rows, 128), jnp.float32),
            pltpu.VMEM((4, 256, 384), jnp.bfloat16),
            pltpu.VMEM((4, 384, 256), jnp.bfloat16),
            pltpu.VMEM((8, 128), jnp.float32),
            pltpu.SemaphoreType.DMA((len(WAYS),)),
            pltpu.SemaphoreType.DMA((len(WAYS),)),
            pltpu.SemaphoreType.DMA((len(WAYS),)),
            pltpu.SemaphoreType.DMA((len(WAYS),)),
            pltpu.SemaphoreType.DMA((fold,)),
            pltpu.SemaphoreType.DMA((fold,)),
            pltpu.SemaphoreType.DMA,
        ],
        compiler_params=pltpu.CompilerParams(
            collective_id=0, has_side_effects=True, vmem_limit_bytes=40 * 1024 * 1024
        ),
    )(contact, *weights)


def solution(mesh):
    in_specs = (P("row", "col"), P(), P(), P(), P(), P(), P(), P(), P())
    return jax.shard_map(
        functools.partial(per_device, mesh.shape["row"], mesh.shape["col"]),
        mesh=mesh,
        in_specs=in_specs,
        out_specs=P("row", "col"),
        check_vma=False,
    )
```

```python
import functools

import jax
import jax.numpy as jnp
from jax import lax
from jax.experimental import pallas as pl
from jax.experimental.pallas import tpu as pltpu
from jax.sharding import PartitionSpec as P

MESH = pl.DeviceIdType.MESH
HALO = 16
SIDE = HALO // 2
BLOCKS = ((1, 2), (4, 8))
SIDES = ((0, -1), (0, 1))
ENDS = ((-1, 0), (1, 0))
CORNERS = ((-1, -1), (-1, 1), (1, -1), (1, 1))
NT = (((1,), (1,)), ((), ()))


def chunk_of(count, most):
    return max(n for n in range(1, most + 1) if count % n == 0)


def kernel(
    rows_of, cols_of,
    contact, fd, fdb, fu, fub, sd, sdb, su, sub,
    out,
    v1, v2, middle, hid1, hid2, first, mirror, wide, flipped, wd, wu, bias,
    send1, recv1, send2, recv2, send_m, recv_m, local_sem,
):
    tile_rows = contact.shape[0]
    pairs = contact.shape[1] // 128
    span = tile_rows + 2 * HALO
    all_pairs = pairs + 2 * SIDE
    square = 2 * pairs
    fold = tile_rows // square
    half_rows, half_pairs = square // 2, pairs // 2
    begin, end = SIDE, SIDE + pairs
    inner = slice(HALO, HALO + tile_rows)
    r = lax.axis_index("row")
    c = lax.axis_index("col")
    up_edge, down_edge = r == 0, r == rows_of - 1
    left_edge, right_edge = c == 0, c == cols_of - 1

    def there(dr, dc):
        return (r + dr >= 0) & (r + dr < rows_of) & (c + dc >= 0) & (c + dc < cols_of)

    mirror_row = lax.div(c, fold)
    peers = [(mirror_row, fold * r + m) for m in range(fold)]
    slot = lax.rem(c, fold)

    def is_me(peer):
        return (peer[0] == r) & (peer[1] == c)

    barrier = pltpu.get_barrier_semaphore()
    greeted = jnp.int32(0)
    for dr, dc in SIDES + ENDS:
        ok = there(dr, dc)
        greeted += ok.astype(jnp.int32)

        @pl.when(ok)
        def _():
            pl.semaphore_signal(barrier, inc=1, device_id=(r + dr, c + dc), device_id_type=MESH)

    for peer in peers:
        other = jnp.logical_not(is_me(peer))
        greeted += other.astype(jnp.int32)

        @pl.when(other)
        def _():
            pl.semaphore_signal(barrier, inc=1, device_id=peer, device_id_type=MESH)

    def clear(buf, low, high, lanes=slice(0, 128)):
        width = lanes.stop - lanes.start
        buf[low:high, :, lanes] = jnp.zeros((high - low, span, width), buf.dtype)

    def clear_rows(buf):
        strip = jnp.zeros((all_pairs, HALO, 128), buf.dtype)

        @pl.when(up_edge)
        def _():
            buf[:, 0:HALO, :] = strip

        @pl.when(down_edge)
        def _():
            buf[:, HALO + tile_rows : span, :] = strip

    def clear_outside(buf):
        clear_rows(buf)

        @pl.when(left_edge)
        def _():
            clear(buf, 0, begin)

        @pl.when(right_edge)
        def _():
            clear(buf, end, all_pairs)

    def clear_hidden(hid, s):
        clear_rows(hid)

        @pl.when(left_edge)
        def _():
            clear(hid, 0, begin, slice(0, 64))
            clear(hid, 0, begin - s, slice(64, 128))

        @pl.when(right_edge)
        def _():
            clear(hid, end, all_pairs, slice(0, 64))
            clear(hid, end - s, all_pairs, slice(64, 128))

    class Halo:
        def __init__(self, buf, send, recv):
            self.copies = {}
            for at, (dr, dc) in enumerate(SIDES + ENDS + CORNERS):
                row, rows, to_row = {
                    -1: (HALO, HALO, HALO + tile_rows), 0: (HALO, tile_rows, HALO), 1: (tile_rows, HALO, 0)
                }[dr]
                if dr == 0:
                    col, cols, to_col = {-1: (begin, SIDE, end), 1: (pairs, SIDE, 0)}[dc]
                else:
                    col, cols = {-1: (0, SIDE), 0: (begin, pairs), 1: (end, SIDE)}[dc]
                    to_col = col
                to_device = (jnp.clip(r + dr, 0, rows_of - 1), c)
                if dr == 0:
                    to_device = (r, jnp.clip(c + dc, 0, cols_of - 1))
                self.copies[dr, dc] = pltpu.make_async_remote_copy(
                    src_ref=buf.at[pl.ds(col, cols), pl.ds(row, rows), :],
                    dst_ref=buf.at[pl.ds(to_col, cols), pl.ds(to_row, rows), :],
                    send_sem=send.at[at],
                    recv_sem=recv.at[at],
                    device_id=to_device,
                    device_id_type=MESH,
                )

        def start(self, dr, dc):
            pl.when(there(dr, dc))(self.copies[dr, dc].start)

        def wait_sent(self, dr, dc):
            pl.when(there(dr, dc))(self.copies[dr, dc].wait_send)

        def wait_side(self, dc):
            pl.when(there(0, -dc))(self.copies[0, dc].wait_recv)

        def wait_end(self, dr):
            pl.when(there(-dr, 0))(self.copies[dr, 0].wait_recv)

        def wait_corner(self, dr, dc):
            pl.when(there(-dr, dc))(self.copies[dr, dc].wait_recv)

    def down(buf, hid, at, d, s, s_up, low, high):
        n = chunk_of(high - low, 8)

        def step(i, carry):
            j = low + i * n
            x = jnp.concatenate(
                [buf[pl.ds(j - s, n)], buf[pl.ds(j, n)], buf[pl.ds(j + s, n)]], axis=-1
            ).reshape(n * span, 384)
            sums = lax.dot_general(x, wd[at], NT, preferred_element_type=jnp.float32)
            outer, central = sums[:, :128], sums[:, 128:]
            h = pltpu.roll(outer, d, 0) + central
            h = h + pltpu.roll(pltpu.roll(outer, 64, 1), n * span - d, 0)
            h = jnp.maximum(h + bias[at : at + 1, :], 0.0)
            moved = pltpu.roll(h, 64, 1)
            hid[pl.ds(j, n), :, 0:64] = h.astype(jnp.bfloat16).reshape(n, span, 128)[:, :, 0:64]
            hid[pl.ds(j - s_up, n), :, 64:128] = moved.astype(jnp.bfloat16).reshape(n, span, 128)[
                :, :, 64:128
            ]
            return carry

        lax.fori_loop(0, (high - low) // n, step, 0)
        clear_hidden(hid, s_up)

    def up(hid, at, d, s, low, high, store):
        n = chunk_of(high - low, 8)

        def step(i, carry):
            j = low + i * n
            x = jnp.concatenate([hid[pl.ds(j - s, n)], hid[pl.ds(j + s, n)]], axis=-1)
            sums = jnp.dot(x.reshape(n * span, 256), wu[at], preferred_element_type=jnp.float32)
            u = pltpu.roll(sums[:, :128], d, 0) + sums[:, 128:256]
            u = u + pltpu.roll(sums[:, 256:], n * span - d, 0)
            u = (u + bias[4 + at : 5 + at, :]).reshape(n, span, 128)
            store(j, n, u)
            return carry

        lax.fori_loop(0, (high - low) // n, step, 0)

    def section(buf, halo, at, store_last):
        (d1, d2), (d3, d4) = BLOCKS
        s1, s2, s3, s4 = max(d1 // 2, 1), d2 // 2, d3 // 2, d4 // 2

        def store(j, n, u):
            v = buf[pl.ds(j, n)].astype(jnp.float32) + u
            middle[pl.ds(j, n)] = v.astype(jnp.bfloat16)

        def one(low, high):
            down(buf, hid1, at, d1, s1, s2, low, high)

        def two(low, high):
            up(hid1, at, d2, s2, low, high, store)
            clear_outside(middle)

        def three(low, high):
            down(middle, hid2, at + 1, d3, s3, s4, low, high)

        t1, t2, t3 = s1, s1 + s2, s1 + s2 + s3
        for dr in (-1, 1):
            halo.wait_end(dr)
        one(begin + t1, end - t1)
        for dc in (-1, 1):
            halo.wait_side(-dc)
            for dr in (-1, 1):
                halo.start(dr, dc)
        two(begin + t2, end - t2)
        three(begin + t3, end - t3)
        for dc in (-1, 1):
            for dr in (-1, 1):
                halo.wait_corner(dr, dc)
            if dc < 0:
                one(t1, begin + t1)
                two(t2, begin + t2)
                three(t3, begin + t3)
            else:
                one(end - t1, all_pairs - t1)
                two(end - t2, all_pairs - t2)
                three(end - t3, all_pairs - t3)
        up(hid2, at + 1, d4, s4, begin, end, store_last)
        for way in SIDES + ENDS + CORNERS:
            halo.wait_sent(*way)

    for j in range(pairs):
        v1[begin + j, inner, :] = contact[:, 128 * j : 128 * (j + 1)]
    pl.semaphore_wait(barrier, greeted)
    halo1 = Halo(v1, send1, recv1)
    halo2 = Halo(v2, send2, recv2)
    for way in SIDES + ENDS:
        halo1.start(*way)

    clear_outside(v1)
    clear_outside(v2)
    for ref in (hid1, hid2, wd, wu, bias):
        ref[...] = jnp.zeros(ref.shape, ref.dtype)
    for sec, (dw, db, uw, ub) in enumerate(((fd, fdb, fu, fub), (sd, sdb, su, sub))):
        for block, (d1, d2) in enumerate(BLOCKS):
            at = 2 * sec + block
            bias[at : at + 1, 0:32] = db[block : block + 1, :]
            bias[at : at + 1, 32:64] = db[block : block + 1, :]
            bias[4 + at : 5 + at, 0:64] = ub[block : block + 1, :]
            bias[4 + at : 5 + at, 64:128] = ub[block : block + 1, :]
            for p in range(3):
                group = (0, 128, 64)[p]
                for q in range(3):
                    for par in range(2):
                        shift = par + (q - 1) * d1
                        third = 1 + (shift // 2 > 0) - (shift // 2 < 0)
                        lane = third * 128 + (shift % 2) * 64
                        row = group + par * 32
                        wd[at, row : row + 32, lane : lane + 64] = dw[block, p, q]
                        row = q * 64 + par * 32
                        lane = p * 128 + par * 64
                        wu[at, row : row + 32, lane : lane + 64] = uw[block, p, q]

    def store_first(j, n, u):
        v = middle[pl.ds(j, n), inner, :].astype(jnp.float32) + u[:, inner, :]
        first[pl.ds(j - begin, n)] = v.astype(jnp.bfloat16)

    section(v1, halo1, 0, store_first)

    mirrors = {}
    for half in range(2):
        for m, peer in enumerate(peers):
            src = first.at[:, pl.ds(m * square + half * half_rows, half_rows), :]
            remote = pltpu.make_async_remote_copy(
                src_ref=src,
                dst_ref=mirror.at[slot, half],
                send_sem=send_m.at[m, half],
                recv_sem=recv_m.at[slot, half],
                device_id=peer,
                device_id_type=MESH,
            )
            here = pltpu.make_async_copy(src, mirror.at[slot, half], local_sem.at[half])
            mirrors[half, m] = (peer, remote, here)
            pl.when(jnp.logical_not(is_me(peer)))(remote.start)
            pl.when(is_me(peer))(here.start)
    low_half = lax.broadcasted_iota(jnp.int32, (pairs, 128), 1) < 64
    for half in range(2):
        for m in range(fold):
            peer, remote, here = mirrors[half, m]
            arrived = pltpu.make_async_remote_copy(
                src_ref=mirror.at[m, half],
                dst_ref=mirror.at[m, half],
                send_sem=send_m.at[m, half],
                recv_sem=recv_m.at[m, half],
                device_id=peer,
                device_id_type=MESH,
            )
            pl.when(jnp.logical_not(is_me(peer)))(arrived.wait_recv)
            pl.when(is_me(peer))(here.wait)
        for m in range(fold):
            at = half * fold + m
            wide[at] = mirror[m, half].astype(jnp.float32).reshape(pairs * half_rows, 128)
            for j in range(half_pairs):
                even = wide[at, pl.ds(2 * j, pairs, stride=half_rows), :]
                odd = wide[at, pl.ds(2 * j + 1, pairs, stride=half_rows), :]
                base = (half * half_pairs + j) * tile_rows + m * square
                flipped[pl.ds(base, pairs, stride=2), :] = jnp.where(
                    low_half, even, pltpu.roll(odd, 64, 1)
                )
                flipped[pl.ds(base + 1, pairs, stride=2), :] = jnp.where(
                    low_half, pltpu.roll(even, 64, 1), odd
                )
        low = half * half_pairs
        own = first[low : low + half_pairs].astype(jnp.float32)
        turned = flipped[low * tile_rows : (low + half_pairs) * tile_rows, :]
        both = (own + turned.reshape(half_pairs, tile_rows, 128)) * 0.5
        v2[begin + low : begin + low + half_pairs, inner, :] = both.astype(jnp.bfloat16)
        if pairs >= 2 * SIDE or half == 1:
            halo2.start(0, 2 * half - 1)
    if pairs < 2 * SIDE:
        halo2.start(0, -1)
    for way in ENDS:
        halo2.start(*way)
    for half in range(2):
        for m in range(fold):
            peer, remote, here = mirrors[half, m]
            pl.when(jnp.logical_not(is_me(peer)))(remote.wait_send)

    def store_second(j, n, u):
        v = (middle[pl.ds(j, n), inner, :].astype(jnp.float32) + u[:, inner, :]).astype(jnp.bfloat16)
        for k in range(n):
            out[:, pl.ds(pl.multiple_of((j - begin + k) * 128, 128), 128)] = v[k]

    section(v2, halo2, 2, store_second)


def per_device(rows_of, cols_of, contact, *weights):
    tile_rows = contact.shape[0]
    pairs = contact.shape[1] // 128
    span, all_pairs, square = tile_rows + 2 * HALO, pairs + 2 * SIDE, 2 * pairs
    fold = tile_rows // square
    ways = len(SIDES + ENDS + CORNERS)
    buf = pltpu.VMEM((all_pairs, span, 128), jnp.bfloat16)
    return pl.pallas_call(
        functools.partial(kernel, rows_of, cols_of),
        out_shape=jax.ShapeDtypeStruct(contact.shape, jnp.bfloat16),
        in_specs=[pl.BlockSpec(memory_space=pltpu.VMEM)] * (1 + len(weights)),
        out_specs=pl.BlockSpec(memory_space=pltpu.VMEM),
        scratch_shapes=[
            buf,
            buf,
            buf,
            buf,
            buf,
            pltpu.VMEM((pairs, tile_rows, 128), jnp.bfloat16),
            pltpu.VMEM((fold, 2, pairs, pairs, 128), jnp.bfloat16),
            pltpu.VMEM((2 * fold, pairs * pairs, 128), jnp.float32),
            pltpu.VMEM((pairs * tile_rows, 128), jnp.float32),
            pltpu.VMEM((4, 256, 384), jnp.bfloat16),
            pltpu.VMEM((4, 256, 384), jnp.bfloat16),
            pltpu.VMEM((8, 128), jnp.float32),
            pltpu.SemaphoreType.DMA((ways,)),
            pltpu.SemaphoreType.DMA((ways,)),
            pltpu.SemaphoreType.DMA((ways,)),
            pltpu.SemaphoreType.DMA((ways,)),
            pltpu.SemaphoreType.DMA((fold, 2)),
            pltpu.SemaphoreType.DMA((fold, 2)),
            pltpu.SemaphoreType.DMA((2,)),
        ],
        compiler_params=pltpu.CompilerParams(
            collective_id=0, has_side_effects=True, vmem_limit_bytes=40 * 1024 * 1024
        ),
    )(contact, *(w.swapaxes(3, 4) if at in (2, 6) else w for at, w in enumerate(weights)))


def solution(mesh):
    in_specs = (P("row", "col"), P(), P(), P(), P(), P(), P(), P(), P())
    return jax.shard_map(
        functools.partial(per_device, mesh.shape["row"], mesh.shape["col"]),
        mesh=mesh,
        in_specs=in_specs,
        out_specs=P("row", "col"),
        check_vma=False,
    )
```

```python
import functools

import jax
import jax.numpy as jnp
from jax import lax
from jax.experimental import pallas as pl
from jax.experimental.pallas import tpu as pltpu
from jax.sharding import PartitionSpec as P

MESH = pl.DeviceIdType.MESH
HALO = 16
SIDE = HALO // 2
BLOCKS = ((1, 2), (4, 8))
SIDES = ((0, -1), (0, 1))
ENDS = ((-1, 0), (1, 0))
CORNERS = ((-1, -1), (-1, 1), (1, -1), (1, 1))
NT = (((1,), (1,)), ((), ()))


def chunk_of(count, most):
    return max(n for n in range(1, most + 1) if count % n == 0)


def kernel(
    rows_of, cols_of,
    contact, *refs,
):
    weights, (out,), held = refs[:8], refs[8:9], refs[9:17]
    (
    v1, v2, middle, hid1, hid2, first, mirror, wide, flipped, wd, wu, bias,
    send1, recv1, send2, recv2, send_m, recv_m, local_sem, load_sem, weight_sem,
    ) = refs[17:]
    fd, fdb, fu, fub, sd, sdb, su, sub = held
    tile_rows = contact.shape[0]
    pairs = contact.shape[1] // 128
    span = tile_rows + 2 * HALO
    all_pairs = pairs + 2 * SIDE
    square = 2 * pairs
    fold = tile_rows // square
    half_rows, half_pairs = square // 2, pairs // 2
    begin, end = SIDE, SIDE + pairs
    inner = slice(HALO, HALO + tile_rows)
    r = lax.axis_index("row")
    c = lax.axis_index("col")
    up_edge, down_edge = r == 0, r == rows_of - 1
    left_edge, right_edge = c == 0, c == cols_of - 1

    def there(dr, dc):
        return (r + dr >= 0) & (r + dr < rows_of) & (c + dc >= 0) & (c + dc < cols_of)

    mirror_row = lax.div(c, fold)
    peers = [(mirror_row, fold * r + m) for m in range(fold)]
    slot = lax.rem(c, fold)

    def is_me(peer):
        return (peer[0] == r) & (peer[1] == c)

    loads = [
        pltpu.make_async_copy(
            contact.at[:, pl.ds(128 * j, 128)],
            v1.at[begin + j, pl.ds(HALO, tile_rows), :],
            load_sem.at[j],
        )
        for j in range(pairs)
    ]
    weight_loads = [
        pltpu.make_async_copy(src, dst, weight_sem.at[at])
        for at, (src, dst) in enumerate(zip(weights, held))
    ]
    for load in loads + weight_loads:
        load.start()

    barrier = pltpu.get_barrier_semaphore()
    greeted = jnp.int32(0)
    for dr, dc in SIDES + ENDS:
        ok = there(dr, dc)
        greeted += ok.astype(jnp.int32)

        @pl.when(ok)
        def _():
            pl.semaphore_signal(barrier, inc=1, device_id=(r + dr, c + dc), device_id_type=MESH)

    for peer in peers:
        other = jnp.logical_not(is_me(peer))
        greeted += other.astype(jnp.int32)

        @pl.when(other)
        def _():
            pl.semaphore_signal(barrier, inc=1, device_id=peer, device_id_type=MESH)

    def clear(buf, low, high, lanes=slice(0, 128)):
        width = lanes.stop - lanes.start
        buf[low:high, :, lanes] = jnp.zeros((high - low, span, width), buf.dtype)

    def clear_rows(buf):
        strip = jnp.zeros((all_pairs, HALO, 128), buf.dtype)

        @pl.when(up_edge)
        def _():
            buf[:, 0:HALO, :] = strip

        @pl.when(down_edge)
        def _():
            buf[:, HALO + tile_rows : span, :] = strip

    def clear_outside(buf):
        clear_rows(buf)

        @pl.when(left_edge)
        def _():
            clear(buf, 0, begin)

        @pl.when(right_edge)
        def _():
            clear(buf, end, all_pairs)

    def clear_hidden(hid, s):
        clear_rows(hid)

        @pl.when(left_edge)
        def _():
            clear(hid, 0, begin, slice(0, 64))
            clear(hid, 0, begin - s, slice(64, 128))

        @pl.when(right_edge)
        def _():
            clear(hid, end, all_pairs, slice(0, 64))
            clear(hid, end - s, all_pairs, slice(64, 128))

    class Halo:
        def __init__(self, buf, send, recv):
            self.copies = {}
            for at, (dr, dc) in enumerate(SIDES + ENDS + CORNERS):
                row, rows, to_row = {
                    -1: (HALO, HALO, HALO + tile_rows), 0: (HALO, tile_rows, HALO), 1: (tile_rows, HALO, 0)
                }[dr]
                if dr == 0:
                    col, cols, to_col = {-1: (begin, SIDE, end), 1: (pairs, SIDE, 0)}[dc]
                else:
                    col, cols = {-1: (0, SIDE), 0: (begin, pairs), 1: (end, SIDE)}[dc]
                    to_col = col
                to_device = (jnp.clip(r + dr, 0, rows_of - 1), c)
                if dr == 0:
                    to_device = (r, jnp.clip(c + dc, 0, cols_of - 1))
                self.copies[dr, dc] = pltpu.make_async_remote_copy(
                    src_ref=buf.at[pl.ds(col, cols), pl.ds(row, rows), :],
                    dst_ref=buf.at[pl.ds(to_col, cols), pl.ds(to_row, rows), :],
                    send_sem=send.at[at],
                    recv_sem=recv.at[at],
                    device_id=to_device,
                    device_id_type=MESH,
                )

        def start(self, dr, dc):
            pl.when(there(dr, dc))(self.copies[dr, dc].start)

        def wait_sent(self, dr, dc):
            pl.when(there(dr, dc))(self.copies[dr, dc].wait_send)

        def wait_side(self, dc):
            pl.when(there(0, -dc))(self.copies[0, dc].wait_recv)

        def wait_end(self, dr):
            pl.when(there(-dr, 0))(self.copies[dr, 0].wait_recv)

        def wait_corner(self, dr, dc):
            pl.when(there(-dr, dc))(self.copies[dr, dc].wait_recv)

    def down(buf, hid, at, d, s, s_up, low, high):
        n = chunk_of(high - low, 8)

        def step(i, carry):
            j = low + i * n
            x = jnp.concatenate(
                [buf[pl.ds(j - s, n)], buf[pl.ds(j, n)], buf[pl.ds(j + s, n)]], axis=-1
            ).reshape(n * span, 384)
            sums = lax.dot_general(x, wd[at], NT, preferred_element_type=jnp.float32)
            outer, central = sums[:, :128], sums[:, 128:]
            h = pltpu.roll(outer, d, 0) + central
            h = h + pltpu.roll(pltpu.roll(outer, 64, 1), n * span - d, 0)
            h = jnp.maximum(h + bias[at : at + 1, :], 0.0)
            moved = pltpu.roll(h, 64, 1)
            hid[pl.ds(j, n), :, 0:64] = h.astype(jnp.bfloat16).reshape(n, span, 128)[:, :, 0:64]
            hid[pl.ds(j - s_up, n), :, 64:128] = moved.astype(jnp.bfloat16).reshape(n, span, 128)[
                :, :, 64:128
            ]
            return carry

        lax.fori_loop(0, (high - low) // n, step, 0)
        clear_hidden(hid, s_up)

    def up(hid, at, d, s, low, high, store):
        n = chunk_of(high - low, 8)

        def step(i, carry):
            j = low + i * n
            x = jnp.concatenate([hid[pl.ds(j - s, n)], hid[pl.ds(j + s, n)]], axis=-1)
            sums = jnp.dot(x.reshape(n * span, 256), wu[at], preferred_element_type=jnp.float32)
            u = pltpu.roll(sums[:, :128], d, 0) + sums[:, 128:256]
            u = u + pltpu.roll(sums[:, 256:], n * span - d, 0)
            u = (u + bias[4 + at : 5 + at, :]).reshape(n, span, 128)
            store(j, n, u)
            return carry

        lax.fori_loop(0, (high - low) // n, step, 0)

    def section(buf, halo, at, store_last):
        (d1, d2), (d3, d4) = BLOCKS
        s1, s2, s3, s4 = max(d1 // 2, 1), d2 // 2, d3 // 2, d4 // 2

        def store(j, n, u):
            v = buf[pl.ds(j, n)].astype(jnp.float32) + u
            middle[pl.ds(j, n)] = v.astype(jnp.bfloat16)

        def one(low, high):
            down(buf, hid1, at, d1, s1, s2, low, high)

        def two(low, high):
            up(hid1, at, d2, s2, low, high, store)
            clear_outside(middle)

        def three(low, high):
            down(middle, hid2, at + 1, d3, s3, s4, low, high)

        t1, t2, t3 = s1, s1 + s2, s1 + s2 + s3
        for dr in (-1, 1):
            halo.wait_end(dr)
        one(begin + t1, end - t1)
        for dc in (-1, 1):
            halo.wait_side(-dc)
            for dr in (-1, 1):
                halo.start(dr, dc)
        two(begin + t2, end - t2)
        three(begin + t3, end - t3)
        for dc in (-1, 1):
            for dr in (-1, 1):
                halo.wait_corner(dr, dc)
            if dc < 0:
                one(t1, begin + t1)
                two(t2, begin + t2)
                three(t3, begin + t3)
            else:
                one(end - t1, all_pairs - t1)
                two(end - t2, all_pairs - t2)
                three(end - t3, all_pairs - t3)
        up(hid2, at + 1, d4, s4, begin, end, store_last)
        for way in SIDES + ENDS + CORNERS:
            halo.wait_sent(*way)

    for load in loads:
        load.wait()
    pl.semaphore_wait(barrier, greeted)
    halo1 = Halo(v1, send1, recv1)
    halo2 = Halo(v2, send2, recv2)
    for way in SIDES + ENDS:
        halo1.start(*way)

    clear_outside(v1)
    clear_outside(v2)
    for ref in (hid1, hid2, wd, wu, bias):
        ref[...] = jnp.zeros(ref.shape, ref.dtype)
    for load in weight_loads:
        load.wait()
    for sec, (dw, db, uw, ub) in enumerate(((fd, fdb, fu, fub), (sd, sdb, su, sub))):
        for block, (d1, d2) in enumerate(BLOCKS):
            at = 2 * sec + block
            bias[at : at + 1, 0:32] = db[block : block + 1, :]
            bias[at : at + 1, 32:64] = db[block : block + 1, :]
            bias[4 + at : 5 + at, 0:64] = ub[block : block + 1, :]
            bias[4 + at : 5 + at, 64:128] = ub[block : block + 1, :]
            for p in range(3):
                group = (0, 128, 64)[p]
                for q in range(3):
                    for par in range(2):
                        shift = par + (q - 1) * d1
                        third = 1 + (shift // 2 > 0) - (shift // 2 < 0)
                        lane = third * 128 + (shift % 2) * 64
                        row = group + par * 32
                        wd[at, row : row + 32, lane : lane + 64] = dw[block, p, q]
                        row = q * 64 + par * 32
                        lane = p * 128 + par * 64
                        wu[at, row : row + 32, lane : lane + 64] = uw[block, p, q]

    def store_first(j, n, u):
        v = middle[pl.ds(j, n), inner, :].astype(jnp.float32) + u[:, inner, :]
        first[pl.ds(j - begin, n)] = v.astype(jnp.bfloat16)

    section(v1, halo1, 0, store_first)

    mirrors = {}
    for half in range(2):
        for m, peer in enumerate(peers):
            src = first.at[:, pl.ds(m * square + half * half_rows, half_rows), :]
            remote = pltpu.make_async_remote_copy(
                src_ref=src,
                dst_ref=mirror.at[slot, half],
                send_sem=send_m.at[m, half],
                recv_sem=recv_m.at[slot, half],
                device_id=peer,
                device_id_type=MESH,
            )
            here = pltpu.make_async_copy(src, mirror.at[slot, half], local_sem.at[half])
            mirrors[half, m] = (peer, remote, here)
            pl.when(jnp.logical_not(is_me(peer)))(remote.start)
            pl.when(is_me(peer))(here.start)
    low_half = lax.broadcasted_iota(jnp.int32, (pairs, 128), 1) < 64
    for half in range(2):
        for m in range(fold):
            peer, remote, here = mirrors[half, m]
            arrived = pltpu.make_async_remote_copy(
                src_ref=mirror.at[m, half],
                dst_ref=mirror.at[m, half],
                send_sem=send_m.at[m, half],
                recv_sem=recv_m.at[m, half],
                device_id=peer,
                device_id_type=MESH,
            )
            pl.when(jnp.logical_not(is_me(peer)))(arrived.wait_recv)
            pl.when(is_me(peer))(here.wait)
        for m in range(fold):
            at = half * fold + m
            wide[at] = mirror[m, half].astype(jnp.float32).reshape(pairs * half_rows, 128)
            for j in range(half_pairs):
                even = wide[at, pl.ds(2 * j, pairs, stride=half_rows), :]
                odd = wide[at, pl.ds(2 * j + 1, pairs, stride=half_rows), :]
                base = (half * half_pairs + j) * tile_rows + m * square
                flipped[pl.ds(base, pairs, stride=2), :] = jnp.where(
                    low_half, even, pltpu.roll(odd, 64, 1)
                )
                flipped[pl.ds(base + 1, pairs, stride=2), :] = jnp.where(
                    low_half, pltpu.roll(even, 64, 1), odd
                )
        low = half * half_pairs
        own = first[low : low + half_pairs].astype(jnp.float32)
        turned = flipped[low * tile_rows : (low + half_pairs) * tile_rows, :]
        both = (own + turned.reshape(half_pairs, tile_rows, 128)) * 0.5
        v2[begin + low : begin + low + half_pairs, inner, :] = both.astype(jnp.bfloat16)
        if pairs >= 2 * SIDE or half == 1:
            halo2.start(0, 2 * half - 1)
    if pairs < 2 * SIDE:
        halo2.start(0, -1)
    for way in ENDS:
        halo2.start(*way)
    for half in range(2):
        for m in range(fold):
            peer, remote, here = mirrors[half, m]
            pl.when(jnp.logical_not(is_me(peer)))(remote.wait_send)

    def store_second(j, n, u):
        v = (middle[pl.ds(j, n), inner, :].astype(jnp.float32) + u[:, inner, :]).astype(jnp.bfloat16)
        for k in range(n):
            out[:, pl.ds(pl.multiple_of((j - begin + k) * 128, 128), 128)] = v[k]

    section(v2, halo2, 2, store_second)


def per_device(rows_of, cols_of, contact, *weights):
    tile_rows = contact.shape[0]
    pairs = contact.shape[1] // 128
    span, all_pairs, square = tile_rows + 2 * HALO, pairs + 2 * SIDE, 2 * pairs
    fold = tile_rows // square
    weights = [w.swapaxes(3, 4) if at in (2, 6) else w for at, w in enumerate(weights)]
    ways = len(SIDES + ENDS + CORNERS)
    buf = pltpu.VMEM((all_pairs, span, 128), jnp.bfloat16)
    return pl.pallas_call(
        functools.partial(kernel, rows_of, cols_of),
        out_shape=jax.ShapeDtypeStruct(contact.shape, jnp.bfloat16),
        in_specs=[pl.BlockSpec(memory_space=pl.ANY)] * (1 + len(weights)),
        out_specs=pl.BlockSpec(memory_space=pltpu.VMEM),
        scratch_shapes=[
            *(pltpu.VMEM(w.shape, w.dtype) for w in weights),
            buf,
            buf,
            buf,
            buf,
            buf,
            pltpu.VMEM((pairs, tile_rows, 128), jnp.bfloat16),
            pltpu.VMEM((fold, 2, pairs, pairs, 128), jnp.bfloat16),
            pltpu.VMEM((2 * fold, pairs * pairs, 128), jnp.float32),
            pltpu.VMEM((pairs * tile_rows, 128), jnp.float32),
            pltpu.VMEM((4, 256, 384), jnp.bfloat16),
            pltpu.VMEM((4, 256, 384), jnp.bfloat16),
            pltpu.VMEM((8, 128), jnp.float32),
            pltpu.SemaphoreType.DMA((ways,)),
            pltpu.SemaphoreType.DMA((ways,)),
            pltpu.SemaphoreType.DMA((ways,)),
            pltpu.SemaphoreType.DMA((ways,)),
            pltpu.SemaphoreType.DMA((fold, 2)),
            pltpu.SemaphoreType.DMA((fold, 2)),
            pltpu.SemaphoreType.DMA((2,)),
            pltpu.SemaphoreType.DMA((pairs,)),
            pltpu.SemaphoreType.DMA((len(weights),)),
        ],
        compiler_params=pltpu.CompilerParams(
            collective_id=0, has_side_effects=True, vmem_limit_bytes=56 * 1024 * 1024
        ),
    )(contact, *weights)


def solution(mesh):
    in_specs = (P("row", "col"), P(), P(), P(), P(), P(), P(), P(), P())
    return jax.shard_map(
        functools.partial(per_device, mesh.shape["row"], mesh.shape["col"]),
        mesh=mesh,
        in_specs=in_specs,
        out_specs=P("row", "col"),
        check_vma=False,
    )
```

```python
import functools

import jax
import jax.numpy as jnp
from jax import lax
from jax.experimental import pallas as pl
from jax.experimental.pallas import tpu as pltpu
from jax.sharding import PartitionSpec as P

MESH = pl.DeviceIdType.MESH
HALO = 16
SIDE = HALO // 2
BLOCKS = ((1, 2), (4, 8))
SIDES = ((0, -1), (0, 1))
ENDS = ((-1, 0), (1, 0))
CORNERS = ((-1, -1), (-1, 1), (1, -1), (1, 1))
NT = (((1,), (1,)), ((), ()))


def chunk_of(count, most):
    return max(n for n in range(1, most + 1) if count % n == 0)


def kernel(
    rows_of, cols_of,
    contact, *refs,
):
    weights, (out,), held = refs[:8], refs[8:9], refs[9:17]
    (
    v1, v2, middle, hid1, hid2, first, mirror, passing, wide, flipped, wd, wu, bias,
    send1, recv1, send2, recv2, send_m, recv_m, pass_recv, pass_send, local_sem, load_sem, weight_sem,
    ) = refs[17:]
    fd, fdb, fu, fub, sd, sdb, su, sub = held
    tile_rows = contact.shape[0]
    pairs = contact.shape[1] // 128
    span = tile_rows + 2 * HALO
    all_pairs = pairs + 2 * SIDE
    square = 2 * pairs
    fold = tile_rows // square
    half_rows, half_pairs = square // 2, pairs // 2
    begin, end = SIDE, SIDE + pairs
    inner = slice(HALO, HALO + tile_rows)
    r = lax.axis_index("row")
    c = lax.axis_index("col")
    up_edge, down_edge = r == 0, r == rows_of - 1
    left_edge, right_edge = c == 0, c == cols_of - 1

    def there(dr, dc):
        return (r + dr >= 0) & (r + dr < rows_of) & (c + dc >= 0) & (c + dc < cols_of)

    mirror_row = lax.div(c, fold)
    peers = [(mirror_row, fold * r + m) for m in range(fold)]
    slot = lax.rem(c, fold)

    def is_me(peer):
        return (peer[0] == r) & (peer[1] == c)

    loads = [
        pltpu.make_async_copy(
            contact.at[:, pl.ds(128 * j, 128)],
            v1.at[begin + j, pl.ds(HALO, tile_rows), :],
            load_sem.at[j],
        )
        for j in range(pairs)
    ]
    weight_loads = [
        pltpu.make_async_copy(src, dst, weight_sem.at[at])
        for at, (src, dst) in enumerate(zip(weights, held))
    ]
    for load in loads + weight_loads:
        load.start()

    barrier = pltpu.get_barrier_semaphore()
    greeted = jnp.int32(0)
    for dr, dc in SIDES + ENDS:
        ok = there(dr, dc)
        greeted += ok.astype(jnp.int32)

        @pl.when(ok)
        def _():
            pl.semaphore_signal(barrier, inc=1, device_id=(r + dr, c + dc), device_id_type=MESH)

    for peer in peers:
        other = jnp.logical_not(is_me(peer))
        greeted += other.astype(jnp.int32)

        @pl.when(other)
        def _():
            pl.semaphore_signal(barrier, inc=1, device_id=peer, device_id_type=MESH)

    on_diagonal = mirror_row == r
    row_relays = [(r, fold * r + m) for m in range(fold)]
    served = [(at, lax.div(jnp.int32(at), fold)) for at in range(cols_of)]

    @pl.when(jnp.logical_not(on_diagonal))
    def _():
        for relay in row_relays + [(mirror_row, c)]:
            pl.semaphore_signal(barrier, inc=1, device_id=relay, device_id_type=MESH)

    @pl.when(on_diagonal)
    def _():
        for at, row in served:

            @pl.when(row != r)
            def _():
                pl.semaphore_signal(barrier, inc=1, device_id=(r, at), device_id_type=MESH)

        for row in range(rows_of):

            @pl.when(row != r)
            def _():
                pl.semaphore_signal(barrier, inc=1, device_id=(row, c), device_id_type=MESH)

    greeted += jnp.where(on_diagonal, cols_of - fold + rows_of - 1, fold + 1)

    def clear(buf, low, high, lanes=slice(0, 128)):
        width = lanes.stop - lanes.start
        buf[low:high, :, lanes] = jnp.zeros((high - low, span, width), buf.dtype)

    def clear_rows(buf):
        strip = jnp.zeros((all_pairs, HALO, 128), buf.dtype)

        @pl.when(up_edge)
        def _():
            buf[:, 0:HALO, :] = strip

        @pl.when(down_edge)
        def _():
            buf[:, HALO + tile_rows : span, :] = strip

    def clear_outside(buf):
        clear_rows(buf)

        @pl.when(left_edge)
        def _():
            clear(buf, 0, begin)

        @pl.when(right_edge)
        def _():
            clear(buf, end, all_pairs)

    def clear_hidden(hid, s):
        clear_rows(hid)

        @pl.when(left_edge)
        def _():
            clear(hid, 0, begin, slice(0, 64))
            clear(hid, 0, begin - s, slice(64, 128))

        @pl.when(right_edge)
        def _():
            clear(hid, end, all_pairs, slice(0, 64))
            clear(hid, end - s, all_pairs, slice(64, 128))

    class Halo:
        def __init__(self, buf, send, recv):
            self.copies = {}
            for at, (dr, dc) in enumerate(SIDES + ENDS + CORNERS):
                row, rows, to_row = {
                    -1: (HALO, HALO, HALO + tile_rows), 0: (HALO, tile_rows, HALO), 1: (tile_rows, HALO, 0)
                }[dr]
                if dr == 0:
                    col, cols, to_col = {-1: (begin, SIDE, end), 1: (pairs, SIDE, 0)}[dc]
                else:
                    col, cols = {-1: (0, SIDE), 0: (begin, pairs), 1: (end, SIDE)}[dc]
                    to_col = col
                to_device = (jnp.clip(r + dr, 0, rows_of - 1), c)
                if dr == 0:
                    to_device = (r, jnp.clip(c + dc, 0, cols_of - 1))
                self.copies[dr, dc] = pltpu.make_async_remote_copy(
                    src_ref=buf.at[pl.ds(col, cols), pl.ds(row, rows), :],
                    dst_ref=buf.at[pl.ds(to_col, cols), pl.ds(to_row, rows), :],
                    send_sem=send.at[at],
                    recv_sem=recv.at[at],
                    device_id=to_device,
                    device_id_type=MESH,
                )

        def start(self, dr, dc):
            pl.when(there(dr, dc))(self.copies[dr, dc].start)

        def wait_sent(self, dr, dc):
            pl.when(there(dr, dc))(self.copies[dr, dc].wait_send)

        def wait_side(self, dc):
            pl.when(there(0, -dc))(self.copies[0, dc].wait_recv)

        def wait_end(self, dr):
            pl.when(there(-dr, 0))(self.copies[dr, 0].wait_recv)

        def wait_corner(self, dr, dc):
            pl.when(there(-dr, dc))(self.copies[dr, dc].wait_recv)

    def down(buf, hid, at, d, s, s_up, low, high):
        n = chunk_of(high - low, 8)

        def step(i, carry):
            j = low + i * n
            x = jnp.concatenate(
                [buf[pl.ds(j - s, n)], buf[pl.ds(j, n)], buf[pl.ds(j + s, n)]], axis=-1
            ).reshape(n * span, 384)
            sums = lax.dot_general(x, wd[at], NT, preferred_element_type=jnp.float32)
            outer, central = sums[:, :128], sums[:, 128:]
            h = pltpu.roll(outer, d, 0) + central
            h = h + pltpu.roll(pltpu.roll(outer, 64, 1), n * span - d, 0)
            h = jnp.maximum(h + bias[at : at + 1, :], 0.0)
            moved = pltpu.roll(h, 64, 1)
            hid[pl.ds(j, n), :, 0:64] = h.astype(jnp.bfloat16).reshape(n, span, 128)[:, :, 0:64]
            hid[pl.ds(j - s_up, n), :, 64:128] = moved.astype(jnp.bfloat16).reshape(n, span, 128)[
                :, :, 64:128
            ]
            return carry

        lax.fori_loop(0, (high - low) // n, step, 0)
        clear_hidden(hid, s_up)

    def up(hid, at, d, s, low, high, store):
        n = chunk_of(high - low, 8)

        def step(i, carry):
            j = low + i * n
            x = jnp.concatenate([hid[pl.ds(j - s, n)], hid[pl.ds(j + s, n)]], axis=-1)
            sums = jnp.dot(x.reshape(n * span, 256), wu[at], preferred_element_type=jnp.float32)
            u = pltpu.roll(sums[:, :128], d, 0) + sums[:, 128:256]
            u = u + pltpu.roll(sums[:, 256:], n * span - d, 0)
            u = (u + bias[4 + at : 5 + at, :]).reshape(n, span, 128)
            store(j, n, u)
            return carry

        lax.fori_loop(0, (high - low) // n, step, 0)

    def section(buf, halo, at, store_last):
        (d1, d2), (d3, d4) = BLOCKS
        s1, s2, s3, s4 = max(d1 // 2, 1), d2 // 2, d3 // 2, d4 // 2

        def store(j, n, u):
            v = buf[pl.ds(j, n)].astype(jnp.float32) + u
            middle[pl.ds(j, n)] = v.astype(jnp.bfloat16)

        def one(low, high):
            down(buf, hid1, at, d1, s1, s2, low, high)

        def two(low, high):
            up(hid1, at, d2, s2, low, high, store)
            clear_outside(middle)

        def three(low, high):
            down(middle, hid2, at + 1, d3, s3, s4, low, high)

        t1, t2, t3 = s1, s1 + s2, s1 + s2 + s3
        for dr in (-1, 1):
            halo.wait_end(dr)
        one(begin + t1, end - t1)
        for dc in (-1, 1):
            halo.wait_side(-dc)
            for dr in (-1, 1):
                halo.start(dr, dc)
        two(begin + t2, end - t2)
        three(begin + t3, end - t3)
        for dc in (-1, 1):
            for dr in (-1, 1):
                halo.wait_corner(dr, dc)
            if dc < 0:
                one(t1, begin + t1)
                two(t2, begin + t2)
                three(t3, begin + t3)
            else:
                one(end - t1, all_pairs - t1)
                two(end - t2, all_pairs - t2)
                three(end - t3, all_pairs - t3)
        up(hid2, at + 1, d4, s4, begin, end, store_last)
        for way in SIDES + ENDS + CORNERS:
            halo.wait_sent(*way)

    for load in loads:
        load.wait()
    pl.semaphore_wait(barrier, greeted)
    halo1 = Halo(v1, send1, recv1)
    halo2 = Halo(v2, send2, recv2)
    for way in SIDES + ENDS:
        halo1.start(*way)

    clear_outside(v1)
    clear_outside(v2)
    for ref in (hid1, hid2, wd, wu, bias):
        ref[...] = jnp.zeros(ref.shape, ref.dtype)
    for load in weight_loads:
        load.wait()
    for sec, (dw, db, uw, ub) in enumerate(((fd, fdb, fu, fub), (sd, sdb, su, sub))):
        for block, (d1, d2) in enumerate(BLOCKS):
            at = 2 * sec + block
            bias[at : at + 1, 0:32] = db[block : block + 1, :]
            bias[at : at + 1, 32:64] = db[block : block + 1, :]
            bias[4 + at : 5 + at, 0:64] = ub[block : block + 1, :]
            bias[4 + at : 5 + at, 64:128] = ub[block : block + 1, :]
            for p in range(3):
                group = (0, 128, 64)[p]
                for q in range(3):
                    for par in range(2):
                        shift = par + (q - 1) * d1
                        third = 1 + (shift // 2 > 0) - (shift // 2 < 0)
                        lane = third * 128 + (shift % 2) * 64
                        row = group + par * 32
                        wd[at, row : row + 32, lane : lane + 64] = dw[block, p, q]
                        row = q * 64 + par * 32
                        lane = p * 128 + par * 64
                        wu[at, row : row + 32, lane : lane + 64] = uw[block, p, q]

    def store_first(j, n, u):
        v = middle[pl.ds(j, n), inner, :].astype(jnp.float32) + u[:, inner, :]
        first[pl.ds(j - begin, n)] = v.astype(jnp.bfloat16)

    section(v1, halo1, 0, store_first)

    mirrors = {}
    for half in range(2):
        for m, peer in enumerate(peers):
            src = first.at[:, pl.ds(m * square + half * half_rows, half_rows), :]
            remote = pltpu.make_async_remote_copy(
                src_ref=src,
                dst_ref=mirror.at[slot, half],
                send_sem=send_m.at[m, half],
                recv_sem=recv_m.at[slot, half],
                device_id=peer,
                device_id_type=MESH,
            )
            here = pltpu.make_async_copy(src, mirror.at[slot, half], local_sem.at[half])
            direct = jnp.logical_not(is_me(peer))
            if half == 1:
                around = pltpu.make_async_remote_copy(
                    src_ref=src,
                    dst_ref=passing.at[c],
                    send_sem=send_m.at[m, half],
                    recv_sem=pass_recv.at[c],
                    device_id=row_relays[m],
                    device_id_type=MESH,
                )
                direct = direct & on_diagonal
                pl.when(jnp.logical_not(on_diagonal))(around.start)
            pl.when(direct)(remote.start)
            pl.when(is_me(peer))(here.start)
            mirrors[half, m] = (peer, remote, here)

    def passed(at, row):
        return pltpu.make_async_remote_copy(
            src_ref=passing.at[at],
            dst_ref=mirror.at[at % fold, 1],
            send_sem=pass_send.at[at],
            recv_sem=recv_m.at[at % fold, 1],
            device_id=(row, c),
            device_id_type=MESH,
        )

    def arriving(at):
        return pltpu.make_async_remote_copy(
            src_ref=passing.at[at],
            dst_ref=passing.at[at],
            send_sem=pass_send.at[at],
            recv_sem=pass_recv.at[at],
            device_id=(r, at),
            device_id_type=MESH,
        )

    @pl.when(on_diagonal)
    def _():
        for at, row in served:

            @pl.when(row != r)
            def _():
                arriving(at).wait_recv()
                passed(at, row).start()

    low_half = lax.broadcasted_iota(jnp.int32, (pairs, 128), 1) < 64
    for half in range(2):
        for m in range(fold):
            peer, remote, here = mirrors[half, m]
            arrived = pltpu.make_async_remote_copy(
                src_ref=mirror.at[m, half],
                dst_ref=mirror.at[m, half],
                send_sem=send_m.at[m, half],
                recv_sem=recv_m.at[m, half],
                device_id=peer,
                device_id_type=MESH,
            )
            pl.when(jnp.logical_not(is_me(peer)))(arrived.wait_recv)
            pl.when(is_me(peer))(here.wait)
        for m in range(fold):
            at = half * fold + m
            wide[at] = mirror[m, half].astype(jnp.float32).reshape(pairs * half_rows, 128)
            for j in range(half_pairs):
                even = wide[at, pl.ds(2 * j, pairs, stride=half_rows), :]
                odd = wide[at, pl.ds(2 * j + 1, pairs, stride=half_rows), :]
                base = (half * half_pairs + j) * tile_rows + m * square
                flipped[pl.ds(base, pairs, stride=2), :] = jnp.where(
                    low_half, even, pltpu.roll(odd, 64, 1)
                )
                flipped[pl.ds(base + 1, pairs, stride=2), :] = jnp.where(
                    low_half, pltpu.roll(even, 64, 1), odd
                )
        low = half * half_pairs
        own = first[low : low + half_pairs].astype(jnp.float32)
        turned = flipped[low * tile_rows : (low + half_pairs) * tile_rows, :]
        both = (own + turned.reshape(half_pairs, tile_rows, 128)) * 0.5
        v2[begin + low : begin + low + half_pairs, inner, :] = both.astype(jnp.bfloat16)
        if pairs >= 2 * SIDE or half == 1:
            halo2.start(0, 2 * half - 1)
    if pairs < 2 * SIDE:
        halo2.start(0, -1)
    for way in ENDS:
        halo2.start(*way)
    for half in range(2):
        for m in range(fold):
            peer, remote, here = mirrors[half, m]
            pl.when(jnp.logical_not(is_me(peer)))(remote.wait_send)

    @pl.when(on_diagonal)
    def _():
        for at, row in served:
            pl.when(row != r)(passed(at, row).wait_send)

    def store_second(j, n, u):
        v = (middle[pl.ds(j, n), inner, :].astype(jnp.float32) + u[:, inner, :]).astype(jnp.bfloat16)
        for k in range(n):
            out[:, pl.ds(pl.multiple_of((j - begin + k) * 128, 128), 128)] = v[k]

    section(v2, halo2, 2, store_second)


def per_device(rows_of, cols_of, contact, *weights):
    tile_rows = contact.shape[0]
    pairs = contact.shape[1] // 128
    span, all_pairs, square = tile_rows + 2 * HALO, pairs + 2 * SIDE, 2 * pairs
    fold = tile_rows // square
    weights = [w.swapaxes(3, 4) if at in (2, 6) else w for at, w in enumerate(weights)]
    ways = len(SIDES + ENDS + CORNERS)
    buf = pltpu.VMEM((all_pairs, span, 128), jnp.bfloat16)
    return pl.pallas_call(
        functools.partial(kernel, rows_of, cols_of),
        out_shape=jax.ShapeDtypeStruct(contact.shape, jnp.bfloat16),
        in_specs=[pl.BlockSpec(memory_space=pl.ANY)] * (1 + len(weights)),
        out_specs=pl.BlockSpec(memory_space=pltpu.VMEM),
        scratch_shapes=[
            *(pltpu.VMEM(w.shape, w.dtype) for w in weights),
            buf,
            buf,
            buf,
            buf,
            buf,
            pltpu.VMEM((pairs, tile_rows, 128), jnp.bfloat16),
            pltpu.VMEM((fold, 2, pairs, pairs, 128), jnp.bfloat16),
            pltpu.VMEM((cols_of, pairs, pairs, 128), jnp.bfloat16),
            pltpu.VMEM((2 * fold, pairs * pairs, 128), jnp.float32),
            pltpu.VMEM((pairs * tile_rows, 128), jnp.float32),
            pltpu.VMEM((4, 256, 384), jnp.bfloat16),
            pltpu.VMEM((4, 256, 384), jnp.bfloat16),
            pltpu.VMEM((8, 128), jnp.float32),
            pltpu.SemaphoreType.DMA((ways,)),
            pltpu.SemaphoreType.DMA((ways,)),
            pltpu.SemaphoreType.DMA((ways,)),
            pltpu.SemaphoreType.DMA((ways,)),
            pltpu.SemaphoreType.DMA((fold, 2)),
            pltpu.SemaphoreType.DMA((fold, 2)),
            pltpu.SemaphoreType.DMA((cols_of,)),
            pltpu.SemaphoreType.DMA((cols_of,)),
            pltpu.SemaphoreType.DMA((2,)),
            pltpu.SemaphoreType.DMA((pairs,)),
            pltpu.SemaphoreType.DMA((len(weights),)),
        ],
        compiler_params=pltpu.CompilerParams(
            collective_id=0, has_side_effects=True, vmem_limit_bytes=56 * 1024 * 1024
        ),
    )(contact, *weights)


def solution(mesh):
    in_specs = (P("row", "col"), P(), P(), P(), P(), P(), P(), P(), P())
    return jax.shard_map(
        functools.partial(per_device, mesh.shape["row"], mesh.shape["col"]),
        mesh=mesh,
        in_specs=in_specs,
        out_specs=P("row", "col"),
        check_vma=False,
    )
```

```python
import functools

import jax
import jax.numpy as jnp
from jax import lax
from jax.experimental import pallas as pl
from jax.experimental.pallas import tpu as pltpu
from jax.sharding import PartitionSpec as P

MESH = pl.DeviceIdType.MESH
HALO = 16
SIDE = HALO // 2
BLOCKS = ((1, 2), (4, 8))
SIDES = ((0, -1), (0, 1))
ENDS = ((-1, 0), (1, 0))
CORNERS = ((-1, -1), (-1, 1), (1, -1), (1, 1))


def chunk_of(count, most):
    return max(n for n in range(1, most + 1) if count % n == 0)


def kernel(
    rows_of, cols_of,
    contact, *refs,
):
    weights, (out,), held = refs[:8], refs[8:9], refs[9:17]
    (
    v1, v2, middle, hid1, hid2, first, mirror, wide, flipped, wide_down, wd, wu, bias,
    send1, recv1, send2, recv2, send_m, recv_m, local_sem, load_sem, weight_sem,
    ) = refs[17:]
    fd, fdb, fu, fub, sd, sdb, su, sub = held
    tile_rows = contact.shape[0]
    pairs = contact.shape[1] // 128
    span = tile_rows + 2 * HALO
    all_pairs = pairs + 2 * SIDE
    square = 2 * pairs
    fold = tile_rows // square
    half_rows, half_pairs = square // 2, pairs // 2
    begin, end = SIDE, SIDE + pairs
    inner = slice(HALO, HALO + tile_rows)
    r = lax.axis_index("row")
    c = lax.axis_index("col")
    up_edge, down_edge = r == 0, r == rows_of - 1
    left_edge, right_edge = c == 0, c == cols_of - 1

    def there(dr, dc):
        return (r + dr >= 0) & (r + dr < rows_of) & (c + dc >= 0) & (c + dc < cols_of)

    mirror_row = lax.div(c, fold)
    peers = [(mirror_row, fold * r + m) for m in range(fold)]
    slot = lax.rem(c, fold)

    def is_me(peer):
        return (peer[0] == r) & (peer[1] == c)

    loads = [
        pltpu.make_async_copy(
            contact.at[:, pl.ds(128 * j, 128)],
            v1.at[begin + j, pl.ds(HALO, tile_rows), :],
            load_sem.at[j],
        )
        for j in range(pairs)
    ]
    weight_loads = [
        pltpu.make_async_copy(src, dst, weight_sem.at[at])
        for at, (src, dst) in enumerate(zip(weights, held))
    ]
    for load in loads + weight_loads:
        load.start()

    barrier = pltpu.get_barrier_semaphore()
    greeted = jnp.int32(0)
    for dr, dc in SIDES + ENDS:
        ok = there(dr, dc)
        greeted += ok.astype(jnp.int32)

        @pl.when(ok)
        def _():
            pl.semaphore_signal(barrier, inc=1, device_id=(r + dr, c + dc), device_id_type=MESH)

    for peer in peers:
        other = jnp.logical_not(is_me(peer))
        greeted += other.astype(jnp.int32)

        @pl.when(other)
        def _():
            pl.semaphore_signal(barrier, inc=1, device_id=peer, device_id_type=MESH)

    def clear(buf, low, high, lanes=slice(0, 128)):
        width = lanes.stop - lanes.start
        buf[low:high, :, lanes] = jnp.zeros((high - low, span, width), buf.dtype)

    def clear_rows(buf):
        strip = jnp.zeros((all_pairs, HALO, 128), buf.dtype)

        @pl.when(up_edge)
        def _():
            buf[:, 0:HALO, :] = strip

        @pl.when(down_edge)
        def _():
            buf[:, HALO + tile_rows : span, :] = strip

    def clear_outside(buf):
        clear_rows(buf)

        @pl.when(left_edge)
        def _():
            clear(buf, 0, begin)

        @pl.when(right_edge)
        def _():
            clear(buf, end, all_pairs)

    def clear_hidden(hid, s):
        clear_rows(hid)

        @pl.when(left_edge)
        def _():
            clear(hid, 0, begin, slice(0, 64))
            clear(hid, 0, begin - s, slice(64, 128))

        @pl.when(right_edge)
        def _():
            clear(hid, end, all_pairs, slice(0, 64))
            clear(hid, end - s, all_pairs, slice(64, 128))

    class Halo:
        def __init__(self, buf, send, recv):
            self.copies = {}
            for at, (dr, dc) in enumerate(SIDES + ENDS + CORNERS):
                row, rows, to_row = {
                    -1: (HALO, HALO, HALO + tile_rows), 0: (HALO, tile_rows, HALO), 1: (tile_rows, HALO, 0)
                }[dr]
                if dr == 0:
                    col, cols, to_col = {-1: (begin, SIDE, end), 1: (pairs, SIDE, 0)}[dc]
                else:
                    col, cols = {-1: (0, SIDE), 0: (begin, pairs), 1: (end, SIDE)}[dc]
                    to_col = col
                to_device = (jnp.clip(r + dr, 0, rows_of - 1), c)
                if dr == 0:
                    to_device = (r, jnp.clip(c + dc, 0, cols_of - 1))
                self.copies[dr, dc] = pltpu.make_async_remote_copy(
                    src_ref=buf.at[pl.ds(col, cols), pl.ds(row, rows), :],
                    dst_ref=buf.at[pl.ds(to_col, cols), pl.ds(to_row, rows), :],
                    send_sem=send.at[at],
                    recv_sem=recv.at[at],
                    device_id=to_device,
                    device_id_type=MESH,
                )

        def start(self, dr, dc):
            pl.when(there(dr, dc))(self.copies[dr, dc].start)

        def wait_sent(self, dr, dc):
            pl.when(there(dr, dc))(self.copies[dr, dc].wait_send)

        def wait_side(self, dc):
            pl.when(there(0, -dc))(self.copies[0, dc].wait_recv)

        def wait_end(self, dr):
            pl.when(there(-dr, 0))(self.copies[dr, 0].wait_recv)

        def wait_corner(self, dr, dc):
            pl.when(there(-dr, dc))(self.copies[dr, dc].wait_recv)

    def down(buf, hid, at, d, s, s_up, chunks):
        low, n, stride, count = chunks

        def step(i, carry):
            j = low + i * stride
            x = jnp.concatenate(
                [buf[pl.ds(j - s, n)], buf[pl.ds(j, n)], buf[pl.ds(j + s, n)]], axis=-1
            ).reshape(n * span, 384)
            sums = jnp.dot(x, wd[at], preferred_element_type=jnp.float32)
            outer, central = sums[:, :128], sums[:, 128:]
            h = pltpu.roll(outer, d, 0) + central
            h = h + pltpu.roll(pltpu.roll(outer, 64, 1), n * span - d, 0)
            h = jnp.maximum(h + bias[at : at + 1, :], 0.0)
            moved = pltpu.roll(h, 64, 1)
            hid[pl.ds(j, n), :, 0:64] = h.astype(jnp.bfloat16).reshape(n, span, 128)[:, :, 0:64]
            hid[pl.ds(j - s_up, n), :, 64:128] = moved.astype(jnp.bfloat16).reshape(n, span, 128)[
                :, :, 64:128
            ]
            return carry

        lax.fori_loop(0, count, step, 0)
        clear_hidden(hid, s_up)

    def up(hid, at, d, s, chunks, store):
        low, n, stride, count = chunks

        def step(i, carry):
            j = low + i * stride
            x = jnp.concatenate([hid[pl.ds(j - s, n)], hid[pl.ds(j + s, n)]], axis=-1)
            sums = jnp.dot(x.reshape(n * span, 256), wu[at], preferred_element_type=jnp.float32)
            u = pltpu.roll(sums[:, :128], d, 0) + sums[:, 128:256]
            u = u + pltpu.roll(sums[:, 256:], n * span - d, 0)
            u = (u + bias[4 + at : 5 + at, :]).reshape(n, span, 128)
            store(j, n, u)
            return carry

        lax.fori_loop(0, count, step, 0)

    def section(buf, halo, at, store_last):
        (d1, d2), (d3, d4) = BLOCKS
        s1, s2, s3, s4 = max(d1 // 2, 1), d2 // 2, d3 // 2, d4 // 2

        def store(j, n, u):
            v = buf[pl.ds(j, n)].astype(jnp.float32) + u
            middle[pl.ds(j, n)] = v.astype(jnp.bfloat16)

        def one(chunks):
            down(buf, hid1, at, d1, s1, s2, chunks)

        def two(chunks):
            up(hid1, at, d2, s2, chunks, store)
            clear_outside(middle)

        def three(chunks):
            down(middle, hid2, at + 1, d3, s3, s4, chunks)

        def centre(t):
            n = chunk_of(pairs - 2 * t, 8)
            return begin + t, n, n, (pairs - 2 * t) // n

        def sides(t):
            return t, SIDE, end - 2 * t, 2

        t1, t2, t3 = s1, s1 + s2, s1 + s2 + s3
        for dr in (-1, 1):
            halo.wait_end(dr)
        one(centre(t1))
        for dc in (-1, 1):
            halo.wait_side(-dc)
            for dr in (-1, 1):
                halo.start(dr, dc)
        two(centre(t2))
        three(centre(t3))
        for dr, dc in CORNERS:
            halo.wait_corner(dr, dc)
        one(sides(t1))
        two(sides(t2))
        three(sides(t3))
        up(hid2, at + 1, d4, s4, centre(0), store_last)
        for way in SIDES + ENDS + CORNERS:
            halo.wait_sent(*way)

    for load in loads:
        load.wait()
    pl.semaphore_wait(barrier, greeted)
    halo1 = Halo(v1, send1, recv1)
    halo2 = Halo(v2, send2, recv2)
    for way in SIDES + ENDS:
        halo1.start(*way)

    clear_outside(v1)
    clear_outside(v2)
    for ref in (hid1, hid2, wu, bias):
        ref[...] = jnp.zeros(ref.shape, ref.dtype)
    for load in weight_loads:
        load.wait()
    for sec, (dw, db, uw, ub) in enumerate(((fd, fdb, fu, fub), (sd, sdb, su, sub))):
        for block, (d1, d2) in enumerate(BLOCKS):
            at = 2 * sec + block
            wide_down[...] = jnp.zeros(wide_down.shape, wide_down.dtype)
            bias[at : at + 1, 0:32] = db[block : block + 1, :]
            bias[at : at + 1, 32:64] = db[block : block + 1, :]
            bias[4 + at : 5 + at, 0:64] = ub[block : block + 1, :]
            bias[4 + at : 5 + at, 64:128] = ub[block : block + 1, :]
            for p in range(3):
                group = (0, 128, 64)[p]
                for q in range(3):
                    for par in range(2):
                        shift = par + (q - 1) * d1
                        third = 1 + (shift // 2 > 0) - (shift // 2 < 0)
                        lane = third * 128 + (shift % 2) * 64
                        row = group + par * 32
                        wide_down[row : row + 32, lane : lane + 64] = dw[block, p, q]
                        row = q * 64 + par * 32
                        lane = p * 128 + par * 64
                        wu[at, row : row + 32, lane : lane + 64] = uw[block, p, q]
            wd[at] = wide_down[...].T

    def store_first(j, n, u):
        v = middle[pl.ds(j, n), inner, :].astype(jnp.float32) + u[:, inner, :]
        first[pl.ds(j - begin, n)] = v.astype(jnp.bfloat16)

    section(v1, halo1, 0, store_first)

    mirrors = {}
    for half in range(2):
        for m, peer in enumerate(peers):
            src = first.at[:, pl.ds(m * square + half * half_rows, half_rows), :]
            remote = pltpu.make_async_remote_copy(
                src_ref=src,
                dst_ref=mirror.at[slot, half],
                send_sem=send_m.at[m, half],
                recv_sem=recv_m.at[slot, half],
                device_id=peer,
                device_id_type=MESH,
            )
            here = pltpu.make_async_copy(src, mirror.at[slot, half], local_sem.at[half])
            mirrors[half, m] = (peer, remote, here)
            pl.when(jnp.logical_not(is_me(peer)))(remote.start)
            pl.when(is_me(peer))(here.start)
    low_half = lax.broadcasted_iota(jnp.int32, (pairs, 128), 1) < 64
    for half in range(2):
        for m in range(fold):
            peer, remote, here = mirrors[half, m]
            arrived = pltpu.make_async_remote_copy(
                src_ref=mirror.at[m, half],
                dst_ref=mirror.at[m, half],
                send_sem=send_m.at[m, half],
                recv_sem=recv_m.at[m, half],
                device_id=peer,
                device_id_type=MESH,
            )
            pl.when(jnp.logical_not(is_me(peer)))(arrived.wait_recv)
            pl.when(is_me(peer))(here.wait)
        for m in range(fold):
            at = half * fold + m
            wide[at] = mirror[m, half].astype(jnp.float32).reshape(pairs * half_rows, 128)
            for j in range(half_pairs):
                even = wide[at, pl.ds(2 * j, pairs, stride=half_rows), :]
                odd = wide[at, pl.ds(2 * j + 1, pairs, stride=half_rows), :]
                base = (half * half_pairs + j) * tile_rows + m * square
                flipped[pl.ds(base, pairs, stride=2), :] = jnp.where(
                    low_half, even, pltpu.roll(odd, 64, 1)
                )
                flipped[pl.ds(base + 1, pairs, stride=2), :] = jnp.where(
                    low_half, pltpu.roll(even, 64, 1), odd
                )
        low = half * half_pairs
        own = first[low : low + half_pairs].astype(jnp.float32)
        turned = flipped[low * tile_rows : (low + half_pairs) * tile_rows, :]
        both = (own + turned.reshape(half_pairs, tile_rows, 128)) * 0.5
        v2[begin + low : begin + low + half_pairs, inner, :] = both.astype(jnp.bfloat16)
        if pairs >= 2 * SIDE or half == 1:
            halo2.start(0, 2 * half - 1)
    if pairs < 2 * SIDE:
        halo2.start(0, -1)
    for way in ENDS:
        halo2.start(*way)
    for half in range(2):
        for m in range(fold):
            peer, remote, here = mirrors[half, m]
            pl.when(jnp.logical_not(is_me(peer)))(remote.wait_send)

    def store_second(j, n, u):
        v = (middle[pl.ds(j, n), inner, :].astype(jnp.float32) + u[:, inner, :]).astype(jnp.bfloat16)
        for k in range(n):
            out[:, pl.ds(pl.multiple_of((j - begin + k) * 128, 128), 128)] = v[k]

    section(v2, halo2, 2, store_second)


def per_device(rows_of, cols_of, contact, *weights):
    tile_rows = contact.shape[0]
    pairs = contact.shape[1] // 128
    span, all_pairs, square = tile_rows + 2 * HALO, pairs + 2 * SIDE, 2 * pairs
    fold = tile_rows // square
    weights = [w.swapaxes(3, 4) if at in (2, 6) else w for at, w in enumerate(weights)]
    ways = len(SIDES + ENDS + CORNERS)
    buf = pltpu.VMEM((all_pairs, span, 128), jnp.bfloat16)
    return pl.pallas_call(
        functools.partial(kernel, rows_of, cols_of),
        out_shape=jax.ShapeDtypeStruct(contact.shape, jnp.bfloat16),
        in_specs=[pl.BlockSpec(memory_space=pl.ANY)] * (1 + len(weights)),
        out_specs=pl.BlockSpec(memory_space=pltpu.VMEM),
        scratch_shapes=[
            *(pltpu.VMEM(w.shape, w.dtype) for w in weights),
            buf,
            buf,
            buf,
            buf,
            buf,
            pltpu.VMEM((pairs, tile_rows, 128), jnp.bfloat16),
            pltpu.VMEM((fold, 2, pairs, pairs, 128), jnp.bfloat16),
            pltpu.VMEM((2 * fold, pairs * pairs, 128), jnp.float32),
            pltpu.VMEM((pairs * tile_rows, 128), jnp.float32),
            pltpu.VMEM((256, 384), jnp.bfloat16),
            pltpu.VMEM((4, 384, 256), jnp.bfloat16),
            pltpu.VMEM((4, 256, 384), jnp.bfloat16),
            pltpu.VMEM((8, 128), jnp.float32),
            pltpu.SemaphoreType.DMA((ways,)),
            pltpu.SemaphoreType.DMA((ways,)),
            pltpu.SemaphoreType.DMA((ways,)),
            pltpu.SemaphoreType.DMA((ways,)),
            pltpu.SemaphoreType.DMA((fold, 2)),
            pltpu.SemaphoreType.DMA((fold, 2)),
            pltpu.SemaphoreType.DMA((2,)),
            pltpu.SemaphoreType.DMA((pairs,)),
            pltpu.SemaphoreType.DMA((len(weights),)),
        ],
        compiler_params=pltpu.CompilerParams(
            collective_id=0, has_side_effects=True, vmem_limit_bytes=56 * 1024 * 1024
        ),
    )(contact, *weights)


def solution(mesh):
    in_specs = (P("row", "col"), P(), P(), P(), P(), P(), P(), P(), P())
    return jax.shard_map(
        functools.partial(per_device, mesh.shape["row"], mesh.shape["col"]),
        mesh=mesh,
        in_specs=in_specs,
        out_specs=P("row", "col"),
        check_vma=False,
    )
```

```python
import functools

import jax
import jax.numpy as jnp
from jax import lax
from jax.experimental import pallas as pl
from jax.experimental.pallas import tpu as pltpu
from jax.sharding import PartitionSpec as P

MESH = pl.DeviceIdType.MESH
HALO = 16
SIDE = HALO // 2
BLOCKS = ((1, 2), (4, 8))
SIDES = ((0, -1), (0, 1))
ENDS = ((-1, 0), (1, 0))
CORNERS = ((-1, -1), (-1, 1), (1, -1), (1, 1))


def chunk_of(count, most):
    return max(n for n in range(1, most + 1) if count % n == 0)


def kernel(
    rows_of, cols_of,
    contact, *refs,
):
    weights, (out,), held = refs[:8], refs[8:9], refs[9:17]
    (
    v1, v2, middle, hid1, hid2, first, mirror, passing, wide, flipped, wide_down, wd, wu, bias,
    send1, recv1, send2, recv2, send_m, recv_m, pass_recv, pass_send, local_sem, load_sem, weight_sem,
    ) = refs[17:]
    fd, fdb, fu, fub, sd, sdb, su, sub = held
    tile_rows = contact.shape[0]
    pairs = contact.shape[1] // 128
    span = tile_rows + 2 * HALO
    all_pairs = pairs + 2 * SIDE
    square = 2 * pairs
    fold = tile_rows // square
    half_rows, half_pairs = square // 2, pairs // 2
    begin, end = SIDE, SIDE + pairs
    inner = slice(HALO, HALO + tile_rows)
    r = lax.axis_index("row")
    c = lax.axis_index("col")
    up_edge, down_edge = r == 0, r == rows_of - 1
    left_edge, right_edge = c == 0, c == cols_of - 1

    def there(dr, dc):
        return (r + dr >= 0) & (r + dr < rows_of) & (c + dc >= 0) & (c + dc < cols_of)

    mirror_row = lax.div(c, fold)
    peers = [(mirror_row, fold * r + m) for m in range(fold)]
    slot = lax.rem(c, fold)

    def is_me(peer):
        return (peer[0] == r) & (peer[1] == c)

    loads = [
        pltpu.make_async_copy(
            contact.at[:, pl.ds(128 * j, 128)],
            v1.at[begin + j, pl.ds(HALO, tile_rows), :],
            load_sem.at[j],
        )
        for j in range(pairs)
    ]
    weight_loads = [
        pltpu.make_async_copy(src, dst, weight_sem.at[at])
        for at, (src, dst) in enumerate(zip(weights, held))
    ]
    for load in loads + weight_loads:
        load.start()

    barrier = pltpu.get_barrier_semaphore()
    greeted = jnp.int32(0)
    for dr, dc in SIDES + ENDS:
        ok = there(dr, dc)
        greeted += ok.astype(jnp.int32)

        @pl.when(ok)
        def _():
            pl.semaphore_signal(barrier, inc=1, device_id=(r + dr, c + dc), device_id_type=MESH)

    for peer in peers:
        other = jnp.logical_not(is_me(peer))
        greeted += other.astype(jnp.int32)

        @pl.when(other)
        def _():
            pl.semaphore_signal(barrier, inc=1, device_id=peer, device_id_type=MESH)

    mine, parity = lax.div(r, 2), lax.rem(r, 2)
    home = lax.div(mirror_row, 2) == mine
    away = jnp.logical_not(home)
    relay = (2 * lax.div(mirror_row, 2) + parity, c)

    @pl.when(away)
    def _():
        pl.semaphore_signal(barrier, inc=1, device_id=relay, device_id_type=MESH)
        for m in range(fold):
            giver = (2 * mine + lax.rem(mirror_row, 2), fold * r + m)
            pl.semaphore_signal(barrier, inc=1, device_id=giver, device_id_type=MESH)

    for i in range(rows_of // 2):

        @pl.when(home & (mine != i))
        def _():
            served = 2 * i + parity
            for partner in [(served, c)] + [(mirror_row, fold * served + m) for m in range(fold)]:
                pl.semaphore_signal(barrier, inc=1, device_id=partner, device_id_type=MESH)

    greeted += jnp.where(home, (rows_of // 2 - 1) * (1 + fold), 1 + fold)

    def clear(buf, low, high, lanes=slice(0, 128)):
        width = lanes.stop - lanes.start
        buf[low:high, :, lanes] = jnp.zeros((high - low, span, width), buf.dtype)

    def clear_rows(buf):
        strip = jnp.zeros((all_pairs, HALO, 128), buf.dtype)

        @pl.when(up_edge)
        def _():
            buf[:, 0:HALO, :] = strip

        @pl.when(down_edge)
        def _():
            buf[:, HALO + tile_rows : span, :] = strip

    def clear_outside(buf):
        clear_rows(buf)

        @pl.when(left_edge)
        def _():
            clear(buf, 0, begin)

        @pl.when(right_edge)
        def _():
            clear(buf, end, all_pairs)

    def clear_hidden(hid, s):
        clear_rows(hid)

        @pl.when(left_edge)
        def _():
            clear(hid, 0, begin, slice(0, 64))
            clear(hid, 0, begin - s, slice(64, 128))

        @pl.when(right_edge)
        def _():
            clear(hid, end, all_pairs, slice(0, 64))
            clear(hid, end - s, all_pairs, slice(64, 128))

    class Halo:
        def __init__(self, buf, send, recv):
            self.copies = {}
            for at, (dr, dc) in enumerate(SIDES + ENDS + CORNERS):
                row, rows, to_row = {
                    -1: (HALO, HALO, HALO + tile_rows), 0: (HALO, tile_rows, HALO), 1: (tile_rows, HALO, 0)
                }[dr]
                if dr == 0:
                    col, cols, to_col = {-1: (begin, SIDE, end), 1: (pairs, SIDE, 0)}[dc]
                else:
                    col, cols = {-1: (0, SIDE), 0: (begin, pairs), 1: (end, SIDE)}[dc]
                    to_col = col
                to_device = (jnp.clip(r + dr, 0, rows_of - 1), c)
                if dr == 0:
                    to_device = (r, jnp.clip(c + dc, 0, cols_of - 1))
                self.copies[dr, dc] = pltpu.make_async_remote_copy(
                    src_ref=buf.at[pl.ds(col, cols), pl.ds(row, rows), :],
                    dst_ref=buf.at[pl.ds(to_col, cols), pl.ds(to_row, rows), :],
                    send_sem=send.at[at],
                    recv_sem=recv.at[at],
                    device_id=to_device,
                    device_id_type=MESH,
                )

        def start(self, dr, dc):
            pl.when(there(dr, dc))(self.copies[dr, dc].start)

        def wait_sent(self, dr, dc):
            pl.when(there(dr, dc))(self.copies[dr, dc].wait_send)

        def wait_side(self, dc):
            pl.when(there(0, -dc))(self.copies[0, dc].wait_recv)

        def wait_end(self, dr):
            pl.when(there(-dr, 0))(self.copies[dr, 0].wait_recv)

        def wait_corner(self, dr, dc):
            pl.when(there(-dr, dc))(self.copies[dr, dc].wait_recv)

    def down(buf, hid, at, d, s, s_up, chunks):
        low, n, stride, count = chunks

        def step(i, carry):
            j = low + i * stride
            x = jnp.concatenate(
                [buf[pl.ds(j - s, n)], buf[pl.ds(j, n)], buf[pl.ds(j + s, n)]], axis=-1
            ).reshape(n * span, 384)
            sums = jnp.dot(x, wd[at], preferred_element_type=jnp.float32)
            outer, central = sums[:, :128], sums[:, 128:]
            h = pltpu.roll(outer, d, 0) + central
            h = h + pltpu.roll(pltpu.roll(outer, 64, 1), n * span - d, 0)
            h = jnp.maximum(h + bias[at : at + 1, :], 0.0)
            moved = pltpu.roll(h, 64, 1)
            hid[pl.ds(j, n), :, 0:64] = h.astype(jnp.bfloat16).reshape(n, span, 128)[:, :, 0:64]
            hid[pl.ds(j - s_up, n), :, 64:128] = moved.astype(jnp.bfloat16).reshape(n, span, 128)[
                :, :, 64:128
            ]
            return carry

        lax.fori_loop(0, count, step, 0)
        clear_hidden(hid, s_up)

    def up(hid, at, d, s, chunks, store):
        low, n, stride, count = chunks

        def step(i, carry):
            j = low + i * stride
            x = jnp.concatenate([hid[pl.ds(j - s, n)], hid[pl.ds(j + s, n)]], axis=-1)
            sums = jnp.dot(x.reshape(n * span, 256), wu[at], preferred_element_type=jnp.float32)
            u = pltpu.roll(sums[:, :128], d, 0) + sums[:, 128:256]
            u = u + pltpu.roll(sums[:, 256:], n * span - d, 0)
            u = (u + bias[4 + at : 5 + at, :]).reshape(n, span, 128)
            store(j, n, u)
            return carry

        lax.fori_loop(0, count, step, 0)

    def section(buf, halo, at, store_last):
        (d1, d2), (d3, d4) = BLOCKS
        s1, s2, s3, s4 = max(d1 // 2, 1), d2 // 2, d3 // 2, d4 // 2

        def store(j, n, u):
            v = buf[pl.ds(j, n)].astype(jnp.float32) + u
            middle[pl.ds(j, n)] = v.astype(jnp.bfloat16)

        def one(chunks):
            down(buf, hid1, at, d1, s1, s2, chunks)

        def two(chunks):
            up(hid1, at, d2, s2, chunks, store)
            clear_outside(middle)

        def three(chunks):
            down(middle, hid2, at + 1, d3, s3, s4, chunks)

        def centre(t):
            n = chunk_of(pairs - 2 * t, 8)
            return begin + t, n, n, (pairs - 2 * t) // n

        def sides(t):
            return t, SIDE, end - 2 * t, 2

        t1, t2, t3 = s1, s1 + s2, s1 + s2 + s3
        for dr in (-1, 1):
            halo.wait_end(dr)
        one(centre(t1))
        for dc in (-1, 1):
            halo.wait_side(-dc)
            for dr in (-1, 1):
                halo.start(dr, dc)
        two(centre(t2))
        three(centre(t3))
        for dr, dc in CORNERS:
            halo.wait_corner(dr, dc)
        one(sides(t1))
        two(sides(t2))
        three(sides(t3))
        up(hid2, at + 1, d4, s4, centre(0), store_last)
        for way in SIDES + ENDS + CORNERS:
            halo.wait_sent(*way)

    for load in loads:
        load.wait()
    pl.semaphore_wait(barrier, greeted)
    halo1 = Halo(v1, send1, recv1)
    halo2 = Halo(v2, send2, recv2)
    for way in SIDES + ENDS:
        halo1.start(*way)

    clear_outside(v1)
    clear_outside(v2)
    for ref in (hid1, hid2, wu, bias):
        ref[...] = jnp.zeros(ref.shape, ref.dtype)
    for load in weight_loads:
        load.wait()
    for sec, (dw, db, uw, ub) in enumerate(((fd, fdb, fu, fub), (sd, sdb, su, sub))):
        for block, (d1, d2) in enumerate(BLOCKS):
            at = 2 * sec + block
            wide_down[...] = jnp.zeros(wide_down.shape, wide_down.dtype)
            bias[at : at + 1, 0:32] = db[block : block + 1, :]
            bias[at : at + 1, 32:64] = db[block : block + 1, :]
            bias[4 + at : 5 + at, 0:64] = ub[block : block + 1, :]
            bias[4 + at : 5 + at, 64:128] = ub[block : block + 1, :]
            for p in range(3):
                group = (0, 128, 64)[p]
                for q in range(3):
                    for par in range(2):
                        shift = par + (q - 1) * d1
                        third = 1 + (shift // 2 > 0) - (shift // 2 < 0)
                        lane = third * 128 + (shift % 2) * 64
                        row = group + par * 32
                        wide_down[row : row + 32, lane : lane + 64] = dw[block, p, q]
                        row = q * 64 + par * 32
                        lane = p * 128 + par * 64
                        wu[at, row : row + 32, lane : lane + 64] = uw[block, p, q]
            wd[at] = wide_down[...].T

    def store_first(j, n, u):
        v = middle[pl.ds(j, n), inner, :].astype(jnp.float32) + u[:, inner, :]
        first[pl.ds(j - begin, n)] = v.astype(jnp.bfloat16)

    section(v1, halo1, 0, store_first)

    def piece(half, m):
        return first.at[:, pl.ds(m * square + half * half_rows, half_rows), :]

    for m in range(fold):

        @pl.when(away)
        def _():
            pltpu.make_async_remote_copy(
                src_ref=piece(1, m),
                dst_ref=passing.at[mine, m],
                send_sem=send_m.at[m, 1],
                recv_sem=pass_recv.at[mine, m],
                device_id=relay,
                device_id_type=MESH,
            ).start()

    mirrors = {}
    for half in range(2):
        for m, peer in enumerate(peers):
            remote = pltpu.make_async_remote_copy(
                src_ref=piece(half, m),
                dst_ref=mirror.at[slot, half],
                send_sem=send_m.at[m, half],
                recv_sem=recv_m.at[slot, half],
                device_id=peer,
                device_id_type=MESH,
            )
            here = pltpu.make_async_copy(piece(half, m), mirror.at[slot, half], local_sem.at[half])
            direct = jnp.logical_not(is_me(peer))
            if half == 1:
                direct = direct & home
            pl.when(direct)(remote.start)
            pl.when(is_me(peer))(here.start)
            mirrors[half, m] = (peer, remote, here)

    def passed(i, m):
        return pltpu.make_async_remote_copy(
            src_ref=passing.at[i, m],
            dst_ref=mirror.at[slot, 1],
            send_sem=pass_send.at[i, m],
            recv_sem=recv_m.at[slot, 1],
            device_id=(mirror_row, fold * (2 * i + parity) + m),
            device_id_type=MESH,
        )

    for i in range(rows_of // 2):

        @pl.when(home & (mine != i))
        def _():
            for m in range(fold):
                pltpu.make_async_remote_copy(
                    src_ref=passing.at[i, m],
                    dst_ref=passing.at[i, m],
                    send_sem=pass_send.at[i, m],
                    recv_sem=pass_recv.at[i, m],
                    device_id=(2 * i + parity, c),
                    device_id_type=MESH,
                ).wait_recv()
                passed(i, m).start()

    low_half = lax.broadcasted_iota(jnp.int32, (pairs, 128), 1) < 64
    for half in range(2):
        for m in range(fold):
            peer, remote, here = mirrors[half, m]
            arrived = pltpu.make_async_remote_copy(
                src_ref=mirror.at[m, half],
                dst_ref=mirror.at[m, half],
                send_sem=send_m.at[m, half],
                recv_sem=recv_m.at[m, half],
                device_id=peer,
                device_id_type=MESH,
            )
            pl.when(jnp.logical_not(is_me(peer)))(arrived.wait_recv)
            pl.when(is_me(peer))(here.wait)
        for m in range(fold):
            at = half * fold + m
            wide[at] = mirror[m, half].astype(jnp.float32).reshape(pairs * half_rows, 128)
            for j in range(half_pairs):
                even = wide[at, pl.ds(2 * j, pairs, stride=half_rows), :]
                odd = wide[at, pl.ds(2 * j + 1, pairs, stride=half_rows), :]
                base = (half * half_pairs + j) * tile_rows + m * square
                flipped[pl.ds(base, pairs, stride=2), :] = jnp.where(
                    low_half, even, pltpu.roll(odd, 64, 1)
                )
                flipped[pl.ds(base + 1, pairs, stride=2), :] = jnp.where(
                    low_half, pltpu.roll(even, 64, 1), odd
                )
        low = half * half_pairs
        own = first[low : low + half_pairs].astype(jnp.float32)
        turned = flipped[low * tile_rows : (low + half_pairs) * tile_rows, :]
        both = (own + turned.reshape(half_pairs, tile_rows, 128)) * 0.5
        v2[begin + low : begin + low + half_pairs, inner, :] = both.astype(jnp.bfloat16)
        if pairs >= 2 * SIDE or half == 1:
            halo2.start(0, 2 * half - 1)
    if pairs < 2 * SIDE:
        halo2.start(0, -1)
    for way in ENDS:
        halo2.start(*way)
    for half in range(2):
        for m in range(fold):
            peer, remote, here = mirrors[half, m]
            pl.when(jnp.logical_not(is_me(peer)))(remote.wait_send)
    for i in range(rows_of // 2):

        @pl.when(home & (mine != i))
        def _():
            for m in range(fold):
                passed(i, m).wait_send()

    def store_second(j, n, u):
        v = (middle[pl.ds(j, n), inner, :].astype(jnp.float32) + u[:, inner, :]).astype(jnp.bfloat16)
        for k in range(n):
            out[:, pl.ds(pl.multiple_of((j - begin + k) * 128, 128), 128)] = v[k]

    section(v2, halo2, 2, store_second)


def per_device(rows_of, cols_of, contact, *weights):
    tile_rows = contact.shape[0]
    pairs = contact.shape[1] // 128
    span, all_pairs, square = tile_rows + 2 * HALO, pairs + 2 * SIDE, 2 * pairs
    fold = tile_rows // square
    weights = [w.swapaxes(3, 4) if at in (2, 6) else w for at, w in enumerate(weights)]
    ways = len(SIDES + ENDS + CORNERS)
    buf = pltpu.VMEM((all_pairs, span, 128), jnp.bfloat16)
    return pl.pallas_call(
        functools.partial(kernel, rows_of, cols_of),
        out_shape=jax.ShapeDtypeStruct(contact.shape, jnp.bfloat16),
        in_specs=[pl.BlockSpec(memory_space=pl.ANY)] * (1 + len(weights)),
        out_specs=pl.BlockSpec(memory_space=pltpu.VMEM),
        scratch_shapes=[
            *(pltpu.VMEM(w.shape, w.dtype) for w in weights),
            buf,
            buf,
            buf,
            buf,
            buf,
            pltpu.VMEM((pairs, tile_rows, 128), jnp.bfloat16),
            pltpu.VMEM((fold, 2, pairs, pairs, 128), jnp.bfloat16),
            pltpu.VMEM((rows_of // 2, fold, pairs, pairs, 128), jnp.bfloat16),
            pltpu.VMEM((2 * fold, pairs * pairs, 128), jnp.float32),
            pltpu.VMEM((pairs * tile_rows, 128), jnp.float32),
            pltpu.VMEM((256, 384), jnp.bfloat16),
            pltpu.VMEM((4, 384, 256), jnp.bfloat16),
            pltpu.VMEM((4, 256, 384), jnp.bfloat16),
            pltpu.VMEM((8, 128), jnp.float32),
            pltpu.SemaphoreType.DMA((ways,)),
            pltpu.SemaphoreType.DMA((ways,)),
            pltpu.SemaphoreType.DMA((ways,)),
            pltpu.SemaphoreType.DMA((ways,)),
            pltpu.SemaphoreType.DMA((fold, 2)),
            pltpu.SemaphoreType.DMA((fold, 2)),
            pltpu.SemaphoreType.DMA((rows_of // 2, fold)),
            pltpu.SemaphoreType.DMA((rows_of // 2, fold)),
            pltpu.SemaphoreType.DMA((2,)),
            pltpu.SemaphoreType.DMA((pairs,)),
            pltpu.SemaphoreType.DMA((len(weights),)),
        ],
        compiler_params=pltpu.CompilerParams(
            collective_id=0, has_side_effects=True, vmem_limit_bytes=56 * 1024 * 1024
        ),
    )(contact, *weights)


def solution(mesh):
    in_specs = (P("row", "col"), P(), P(), P(), P(), P(), P(), P(), P())
    return jax.shard_map(
        functools.partial(per_device, mesh.shape["row"], mesh.shape["col"]),
        mesh=mesh,
        in_specs=in_specs,
        out_specs=P("row", "col"),
        check_vma=False,
    )
```

```python
import functools

import jax
import jax.numpy as jnp
from jax import lax
from jax.experimental import pallas as pl
from jax.experimental.pallas import tpu as pltpu
from jax.sharding import PartitionSpec as P

MESH = pl.DeviceIdType.MESH
HALO = 16
SIDE = HALO // 2
BLOCKS = ((1, 2), (4, 8))
SIDES = ((0, -1), (0, 1))
PARTS = (-1, 1, 0)
ENDS = ((-1, 0), (1, 0))
CORNERS = ((-1, -1), (-1, 1), (1, -1), (1, 1))


def chunk_of(count, most):
    return max(n for n in range(1, most + 1) if count % n == 0)


def kernel(
    rows_of, cols_of,
    contact, *refs,
):
    weights, (out,), held = refs[:8], refs[8:9], refs[9:17]
    (
    v1, v2, middle, hid1, hid2, first, mirror, passing, wide, flipped, wide_down, wd, wu, bias,
    send1, recv1, send2, recv2, send_m, recv_m, pass_recv, pass_send, local_sem, load_sem, weight_sem,
    ) = refs[17:]
    fd, fdb, fu, fub, sd, sdb, su, sub = held
    tile_rows = contact.shape[0]
    pairs = contact.shape[1] // 128
    span = tile_rows + 2 * HALO
    all_pairs = pairs + 2 * SIDE
    square = 2 * pairs
    fold = tile_rows // square
    half_rows, half_pairs = square // 2, pairs // 2
    begin, end = SIDE, SIDE + pairs
    inner = slice(HALO, HALO + tile_rows)
    r = lax.axis_index("row")
    c = lax.axis_index("col")
    up_edge, down_edge = r == 0, r == rows_of - 1
    left_edge, right_edge = c == 0, c == cols_of - 1

    def there(dr, dc):
        return (r + dr >= 0) & (r + dr < rows_of) & (c + dc >= 0) & (c + dc < cols_of)

    mirror_row = lax.div(c, fold)
    peers = [(mirror_row, fold * r + m) for m in range(fold)]
    slot = lax.rem(c, fold)

    def is_me(peer):
        return (peer[0] == r) & (peer[1] == c)

    loads = [
        pltpu.make_async_copy(
            contact.at[:, pl.ds(128 * j, 128)],
            v1.at[begin + j, pl.ds(HALO, tile_rows), :],
            load_sem.at[j],
        )
        for j in range(pairs)
    ]
    weight_loads = [
        pltpu.make_async_copy(src, dst, weight_sem.at[at])
        for at, (src, dst) in enumerate(zip(weights, held))
    ]
    for load in loads + weight_loads:
        load.start()

    barrier = pltpu.get_barrier_semaphore()
    greeted = jnp.int32(0)
    for dr, dc in SIDES + ENDS:
        ok = there(dr, dc)
        greeted += ok.astype(jnp.int32)

        @pl.when(ok)
        def _():
            pl.semaphore_signal(barrier, inc=1, device_id=(r + dr, c + dc), device_id_type=MESH)

    for peer in peers:
        other = jnp.logical_not(is_me(peer))
        greeted += other.astype(jnp.int32)

        @pl.when(other)
        def _():
            pl.semaphore_signal(barrier, inc=1, device_id=peer, device_id_type=MESH)

    mine, parity = lax.div(r, 2), lax.rem(r, 2)
    home = lax.div(mirror_row, 2) == mine
    away = jnp.logical_not(home)
    relay = (2 * lax.div(mirror_row, 2) + parity, c)

    @pl.when(away)
    def _():
        pl.semaphore_signal(barrier, inc=1, device_id=relay, device_id_type=MESH)
        for m in range(fold):
            giver = (2 * mine + lax.rem(mirror_row, 2), fold * r + m)
            pl.semaphore_signal(barrier, inc=1, device_id=giver, device_id_type=MESH)

    for i in range(rows_of // 2):

        @pl.when(home & (mine != i))
        def _():
            served = 2 * i + parity
            for partner in [(served, c)] + [(mirror_row, fold * served + m) for m in range(fold)]:
                pl.semaphore_signal(barrier, inc=1, device_id=partner, device_id_type=MESH)

    greeted += jnp.where(home, (rows_of // 2 - 1) * (1 + fold), 1 + fold)

    def clear(buf, low, high, lanes=slice(0, 128)):
        width = lanes.stop - lanes.start
        buf[low:high, :, lanes] = jnp.zeros((high - low, span, width), buf.dtype)

    def clear_rows(buf):
        strip = jnp.zeros((all_pairs, HALO, 128), buf.dtype)

        @pl.when(up_edge)
        def _():
            buf[:, 0:HALO, :] = strip

        @pl.when(down_edge)
        def _():
            buf[:, HALO + tile_rows : span, :] = strip

    def clear_outside(buf):
        clear_rows(buf)

        @pl.when(left_edge)
        def _():
            clear(buf, 0, begin)

        @pl.when(right_edge)
        def _():
            clear(buf, end, all_pairs)

    def clear_hidden(hid, s):
        clear_rows(hid)

        @pl.when(left_edge)
        def _():
            clear(hid, 0, begin, slice(0, 64))
            clear(hid, 0, begin - s, slice(64, 128))

        @pl.when(right_edge)
        def _():
            clear(hid, end, all_pairs, slice(0, 64))
            clear(hid, end - s, all_pairs, slice(64, 128))

    class Halo:
        def __init__(self, buf, send, recv):
            self.copies = {}
            for at, (dr, dc) in enumerate(ENDS + CORNERS):
                row, to_row = (HALO, HALO + tile_rows) if dr < 0 else (tile_rows, 0)
                col, cols = {-1: (0, SIDE), 0: (begin, pairs), 1: (end, SIDE)}[dc]
                self.copies[dr, dc] = pltpu.make_async_remote_copy(
                    src_ref=buf.at[pl.ds(col, cols), pl.ds(row, HALO), :],
                    dst_ref=buf.at[pl.ds(col, cols), pl.ds(to_row, HALO), :],
                    send_sem=send.at[at],
                    recv_sem=recv.at[at],
                    device_id=(jnp.clip(r + dr, 0, rows_of - 1), c),
                    device_id_type=MESH,
                )
            at = len(ENDS + CORNERS)
            for _, dc in SIDES:
                col, to_col = (begin, end) if dc < 0 else (pairs, 0)
                for part in PARTS:
                    row, rows = {
                        -1: (HALO, HALO), 0: (2 * HALO, tile_rows - 2 * HALO), 1: (tile_rows, HALO)
                    }[part]
                    self.copies[0, dc, part] = pltpu.make_async_remote_copy(
                        src_ref=buf.at[pl.ds(col, SIDE), pl.ds(row, rows), :],
                        dst_ref=buf.at[pl.ds(to_col, SIDE), pl.ds(row, rows), :],
                        send_sem=send.at[at],
                        recv_sem=recv.at[at],
                        device_id=(r, jnp.clip(c + dc, 0, cols_of - 1)),
                        device_id_type=MESH,
                    )
                    at += 1

        def start(self, dr, dc):
            pl.when(there(dr, dc))(self.copies[dr, dc].start)

        def wait_sent(self, dr, dc):
            pl.when(there(dr, dc))(self.copies[dr, dc].wait_send)

        def start_side(self, dc, part):
            pl.when(there(0, dc))(self.copies[0, dc, part].start)

        def wait_side_sent(self, dc, part):
            pl.when(there(0, dc))(self.copies[0, dc, part].wait_send)

        def wait_side(self, dc, part):
            pl.when(there(0, -dc))(self.copies[0, dc, part].wait_recv)

        def wait_end(self, dr):
            pl.when(there(-dr, 0))(self.copies[dr, 0].wait_recv)

        def wait_corner(self, dr, dc):
            pl.when(there(-dr, dc))(self.copies[dr, dc].wait_recv)

    def down(buf, hid, at, d, s, s_up, chunks):
        low, n, stride, count = chunks

        def step(i, carry):
            j = low + i * stride
            x = jnp.concatenate(
                [buf[pl.ds(j - s, n)], buf[pl.ds(j, n)], buf[pl.ds(j + s, n)]], axis=-1
            ).reshape(n * span, 384)
            sums = jnp.dot(x, wd[at], preferred_element_type=jnp.float32)
            outer, central = sums[:, :128], sums[:, 128:]
            h = pltpu.roll(outer, d, 0) + central
            h = h + pltpu.roll(pltpu.roll(outer, 64, 1), n * span - d, 0)
            h = jnp.maximum(h + bias[at : at + 1, :], 0.0)
            moved = pltpu.roll(h, 64, 1)
            hid[pl.ds(j, n), :, 0:64] = h.astype(jnp.bfloat16).reshape(n, span, 128)[:, :, 0:64]
            hid[pl.ds(j - s_up, n), :, 64:128] = moved.astype(jnp.bfloat16).reshape(n, span, 128)[
                :, :, 64:128
            ]
            return carry

        lax.fori_loop(0, count, step, 0)
        clear_hidden(hid, s_up)

    def up(hid, at, d, s, chunks, store):
        low, n, stride, count = chunks

        def step(i, carry):
            j = low + i * stride
            x = jnp.concatenate([hid[pl.ds(j - s, n)], hid[pl.ds(j + s, n)]], axis=-1)
            sums = jnp.dot(x.reshape(n * span, 256), wu[at], preferred_element_type=jnp.float32)
            u = pltpu.roll(sums[:, :128], d, 0) + sums[:, 128:256]
            u = u + pltpu.roll(sums[:, 256:], n * span - d, 0)
            u = (u + bias[4 + at : 5 + at, :]).reshape(n, span, 128)
            store(j, n, u)
            return carry

        lax.fori_loop(0, count, step, 0)

    def section(buf, halo, at, store_last):
        (d1, d2), (d3, d4) = BLOCKS
        s1, s2, s3, s4 = max(d1 // 2, 1), d2 // 2, d3 // 2, d4 // 2

        def store(j, n, u):
            v = buf[pl.ds(j, n)].astype(jnp.float32) + u
            middle[pl.ds(j, n)] = v.astype(jnp.bfloat16)

        def one(chunks):
            down(buf, hid1, at, d1, s1, s2, chunks)

        def two(chunks):
            up(hid1, at, d2, s2, chunks, store)
            clear_outside(middle)

        def three(chunks):
            down(middle, hid2, at + 1, d3, s3, s4, chunks)

        def centre(t):
            n = chunk_of(pairs - 2 * t, 8)
            return begin + t, n, n, (pairs - 2 * t) // n

        def sides(t):
            return t, SIDE, end - 2 * t, 2

        t1, t2, t3 = s1, s1 + s2, s1 + s2 + s3
        for dr in (-1, 1):
            halo.wait_end(dr)
        one(centre(t1))
        for dc in (-1, 1):
            for dr in (-1, 1):
                halo.wait_side(-dc, dr)
                halo.start(dr, dc)
        two(centre(t2))
        three(centre(t3))
        for dc in (-1, 1):
            halo.wait_side(dc, 0)
        for dr, dc in CORNERS:
            halo.wait_corner(dr, dc)
        one(sides(t1))
        two(sides(t2))
        three(sides(t3))
        up(hid2, at + 1, d4, s4, centre(0), store_last)
        for way in ENDS + CORNERS:
            halo.wait_sent(*way)
        for _, dc in SIDES:
            for part in PARTS:
                halo.wait_side_sent(dc, part)

    for load in loads:
        load.wait()
    pl.semaphore_wait(barrier, greeted)
    halo1 = Halo(v1, send1, recv1)
    halo2 = Halo(v2, send2, recv2)
    for way in ENDS:
        halo1.start(*way)
    for part in PARTS:
        for _, dc in SIDES:
            halo1.start_side(dc, part)

    clear_outside(v1)
    clear_outside(v2)
    for ref in (hid1, hid2, wu, bias):
        ref[...] = jnp.zeros(ref.shape, ref.dtype)
    for load in weight_loads:
        load.wait()
    for sec, (dw, db, uw, ub) in enumerate(((fd, fdb, fu, fub), (sd, sdb, su, sub))):
        for block, (d1, d2) in enumerate(BLOCKS):
            at = 2 * sec + block
            wide_down[...] = jnp.zeros(wide_down.shape, wide_down.dtype)
            bias[at : at + 1, 0:32] = db[block : block + 1, :]
            bias[at : at + 1, 32:64] = db[block : block + 1, :]
            bias[4 + at : 5 + at, 0:64] = ub[block : block + 1, :]
            bias[4 + at : 5 + at, 64:128] = ub[block : block + 1, :]
            for p in range(3):
                group = (0, 128, 64)[p]
                for q in range(3):
                    for par in range(2):
                        shift = par + (q - 1) * d1
                        third = 1 + (shift // 2 > 0) - (shift // 2 < 0)
                        lane = third * 128 + (shift % 2) * 64
                        row = group + par * 32
                        wide_down[row : row + 32, lane : lane + 64] = dw[block, p, q]
                        row = q * 64 + par * 32
                        lane = p * 128 + par * 64
                        wu[at, row : row + 32, lane : lane + 64] = uw[block, p, q]
            wd[at] = wide_down[...].T

    def store_first(j, n, u):
        v = middle[pl.ds(j, n), inner, :].astype(jnp.float32) + u[:, inner, :]
        first[pl.ds(j - begin, n)] = v.astype(jnp.bfloat16)

    section(v1, halo1, 0, store_first)

    def piece(half, m):
        return first.at[:, pl.ds(m * square + half * half_rows, half_rows), :]

    for m in range(fold):

        @pl.when(away)
        def _():
            pltpu.make_async_remote_copy(
                src_ref=piece(1, m),
                dst_ref=passing.at[mine, m],
                send_sem=send_m.at[m, 1],
                recv_sem=pass_recv.at[mine, m],
                device_id=relay,
                device_id_type=MESH,
            ).start()

    mirrors = {}
    for half in range(2):
        for m, peer in enumerate(peers):
            remote = pltpu.make_async_remote_copy(
                src_ref=piece(half, m),
                dst_ref=mirror.at[slot, half],
                send_sem=send_m.at[m, half],
                recv_sem=recv_m.at[slot, half],
                device_id=peer,
                device_id_type=MESH,
            )
            here = pltpu.make_async_copy(piece(half, m), mirror.at[slot, half], local_sem.at[half])
            direct = jnp.logical_not(is_me(peer))
            if half == 1:
                direct = direct & home
            pl.when(direct)(remote.start)
            pl.when(is_me(peer))(here.start)
            mirrors[half, m] = (peer, remote, here)

    def passed(i, m):
        return pltpu.make_async_remote_copy(
            src_ref=passing.at[i, m],
            dst_ref=mirror.at[slot, 1],
            send_sem=pass_send.at[i, m],
            recv_sem=recv_m.at[slot, 1],
            device_id=(mirror_row, fold * (2 * i + parity) + m),
            device_id_type=MESH,
        )

    for i in range(rows_of // 2):

        @pl.when(home & (mine != i))
        def _():
            for m in range(fold):
                pltpu.make_async_remote_copy(
                    src_ref=passing.at[i, m],
                    dst_ref=passing.at[i, m],
                    send_sem=pass_send.at[i, m],
                    recv_sem=pass_recv.at[i, m],
                    device_id=(2 * i + parity, c),
                    device_id_type=MESH,
                ).wait_recv()
                passed(i, m).start()

    low_half = lax.broadcasted_iota(jnp.int32, (pairs, 128), 1) < 64
    for half in range(2):
        for m in range(fold):
            peer, remote, here = mirrors[half, m]
            arrived = pltpu.make_async_remote_copy(
                src_ref=mirror.at[m, half],
                dst_ref=mirror.at[m, half],
                send_sem=send_m.at[m, half],
                recv_sem=recv_m.at[m, half],
                device_id=peer,
                device_id_type=MESH,
            )
            pl.when(jnp.logical_not(is_me(peer)))(arrived.wait_recv)
            pl.when(is_me(peer))(here.wait)
        for m in range(fold):
            at = half * fold + m
            wide[at] = mirror[m, half].astype(jnp.float32).reshape(pairs * half_rows, 128)
            for j in range(half_pairs):
                even = wide[at, pl.ds(2 * j, pairs, stride=half_rows), :]
                odd = wide[at, pl.ds(2 * j + 1, pairs, stride=half_rows), :]
                base = (half * half_pairs + j) * tile_rows + m * square
                flipped[pl.ds(base, pairs, stride=2), :] = jnp.where(
                    low_half, even, pltpu.roll(odd, 64, 1)
                )
                flipped[pl.ds(base + 1, pairs, stride=2), :] = jnp.where(
                    low_half, pltpu.roll(even, 64, 1), odd
                )
        low = half * half_pairs
        own = first[low : low + half_pairs].astype(jnp.float32)
        turned = flipped[low * tile_rows : (low + half_pairs) * tile_rows, :]
        both = (own + turned.reshape(half_pairs, tile_rows, 128)) * 0.5
        v2[begin + low : begin + low + half_pairs, inner, :] = both.astype(jnp.bfloat16)
        for part in PARTS:
            halo2.start_side(2 * half - 1, part)
    for way in ENDS:
        halo2.start(*way)
    for half in range(2):
        for m in range(fold):
            peer, remote, here = mirrors[half, m]
            pl.when(jnp.logical_not(is_me(peer)))(remote.wait_send)
    for i in range(rows_of // 2):

        @pl.when(home & (mine != i))
        def _():
            for m in range(fold):
                passed(i, m).wait_send()

    def store_second(j, n, u):
        v = (middle[pl.ds(j, n), inner, :].astype(jnp.float32) + u[:, inner, :]).astype(jnp.bfloat16)
        for k in range(n):
            out[:, pl.ds(pl.multiple_of((j - begin + k) * 128, 128), 128)] = v[k]

    section(v2, halo2, 2, store_second)


def per_device(rows_of, cols_of, contact, *weights):
    tile_rows = contact.shape[0]
    pairs = contact.shape[1] // 128
    span, all_pairs, square = tile_rows + 2 * HALO, pairs + 2 * SIDE, 2 * pairs
    fold = tile_rows // square
    weights = [w.swapaxes(3, 4) if at in (2, 6) else w for at, w in enumerate(weights)]
    ways = len(SIDES) * len(PARTS) + len(ENDS + CORNERS)
    buf = pltpu.VMEM((all_pairs, span, 128), jnp.bfloat16)
    return pl.pallas_call(
        functools.partial(kernel, rows_of, cols_of),
        out_shape=jax.ShapeDtypeStruct(contact.shape, jnp.bfloat16),
        in_specs=[pl.BlockSpec(memory_space=pl.ANY)] * (1 + len(weights)),
        out_specs=pl.BlockSpec(memory_space=pltpu.VMEM),
        scratch_shapes=[
            *(pltpu.VMEM(w.shape, w.dtype) for w in weights),
            buf,
            buf,
            buf,
            buf,
            buf,
            pltpu.VMEM((pairs, tile_rows, 128), jnp.bfloat16),
            pltpu.VMEM((fold, 2, pairs, pairs, 128), jnp.bfloat16),
            pltpu.VMEM((rows_of // 2, fold, pairs, pairs, 128), jnp.bfloat16),
            pltpu.VMEM((2 * fold, pairs * pairs, 128), jnp.float32),
            pltpu.VMEM((pairs * tile_rows, 128), jnp.float32),
            pltpu.VMEM((256, 384), jnp.bfloat16),
            pltpu.VMEM((4, 384, 256), jnp.bfloat16),
            pltpu.VMEM((4, 256, 384), jnp.bfloat16),
            pltpu.VMEM((8, 128), jnp.float32),
            pltpu.SemaphoreType.DMA((ways,)),
            pltpu.SemaphoreType.DMA((ways,)),
            pltpu.SemaphoreType.DMA((ways,)),
            pltpu.SemaphoreType.DMA((ways,)),
            pltpu.SemaphoreType.DMA((fold, 2)),
            pltpu.SemaphoreType.DMA((fold, 2)),
            pltpu.SemaphoreType.DMA((rows_of // 2, fold)),
            pltpu.SemaphoreType.DMA((rows_of // 2, fold)),
            pltpu.SemaphoreType.DMA((2,)),
            pltpu.SemaphoreType.DMA((pairs,)),
            pltpu.SemaphoreType.DMA((len(weights),)),
        ],
        compiler_params=pltpu.CompilerParams(
            collective_id=0, has_side_effects=True, vmem_limit_bytes=56 * 1024 * 1024
        ),
    )(contact, *weights)


def solution(mesh):
    in_specs = (P("row", "col"), P(), P(), P(), P(), P(), P(), P(), P())
    return jax.shard_map(
        functools.partial(per_device, mesh.shape["row"], mesh.shape["col"]),
        mesh=mesh,
        in_specs=in_specs,
        out_specs=P("row", "col"),
        check_vma=False,
    )
```

```python
import functools

import jax
import jax.numpy as jnp
from jax import lax
from jax.experimental import pallas as pl
from jax.experimental.pallas import tpu as pltpu
from jax.sharding import PartitionSpec as P

MESH = pl.DeviceIdType.MESH
HALO = 16
SIDE = HALO // 2
BLOCKS = ((1, 2), (4, 8))
SIDES = ((0, -1), (0, 1))
PARTS = (-1, 1, 0)
ENDS = ((-1, 0), (1, 0))
CORNERS = ((-1, -1), (-1, 1), (1, -1), (1, 1))


def chunk_of(count, most):
    return max(n for n in range(1, most + 1) if count % n == 0)


def kernel(
    rows_of, cols_of,
    contact, *refs,
):
    weights, (out,), held = refs[:8], refs[8:9], refs[9:17]
    (
    v1, v2, middle, hid1, hid2, first, mirror, passing, wide, flipped, wide_down, wd, wu, bias,
    send1, recv1, send2, recv2, send_m, recv_m, pass_recv, pass_send, local_sem, load_sem, weight_sem,
    ) = refs[17:]
    fd, fdb, fu, fub, sd, sdb, su, sub = held
    tile_rows = contact.shape[0]
    pairs = contact.shape[1] // 128
    span = tile_rows + 2 * HALO
    all_pairs = pairs + 2 * SIDE
    square = 2 * pairs
    fold = tile_rows // square
    half_rows, half_pairs = square // 2, pairs // 2
    begin, end = SIDE, SIDE + pairs
    inner = slice(HALO, HALO + tile_rows)
    r = lax.axis_index("row")
    c = lax.axis_index("col")
    up_edge, down_edge = r == 0, r == rows_of - 1
    left_edge, right_edge = c == 0, c == cols_of - 1

    def there(dr, dc):
        return (r + dr >= 0) & (r + dr < rows_of) & (c + dc >= 0) & (c + dc < cols_of)

    mirror_row = lax.div(c, fold)
    peers = [(mirror_row, fold * r + m) for m in range(fold)]
    slot = lax.rem(c, fold)

    def is_me(peer):
        return (peer[0] == r) & (peer[1] == c)

    barrier = pltpu.get_barrier_semaphore()
    greeted = jnp.int32(0)
    for dr, dc in SIDES + ENDS:
        ok = there(dr, dc)
        greeted += ok.astype(jnp.int32)

        @pl.when(ok)
        def _():
            pl.semaphore_signal(barrier, inc=1, device_id=(r + dr, c + dc), device_id_type=MESH)

    for peer in peers:
        other = jnp.logical_not(is_me(peer))
        greeted += other.astype(jnp.int32)

        @pl.when(other)
        def _():
            pl.semaphore_signal(barrier, inc=1, device_id=peer, device_id_type=MESH)

    mine, parity = lax.div(r, 2), lax.rem(r, 2)
    home = lax.div(mirror_row, 2) == mine
    away = jnp.logical_not(home)
    relay = (2 * lax.div(mirror_row, 2) + parity, c)

    @pl.when(away)
    def _():
        pl.semaphore_signal(barrier, inc=1, device_id=relay, device_id_type=MESH)
        for m in range(fold):
            giver = (2 * mine + lax.rem(mirror_row, 2), fold * r + m)
            pl.semaphore_signal(barrier, inc=1, device_id=giver, device_id_type=MESH)

    for i in range(rows_of // 2):

        @pl.when(home & (mine != i))
        def _():
            served = 2 * i + parity
            for partner in [(served, c)] + [(mirror_row, fold * served + m) for m in range(fold)]:
                pl.semaphore_signal(barrier, inc=1, device_id=partner, device_id_type=MESH)

    greeted += jnp.where(home, (rows_of // 2 - 1) * (1 + fold), 1 + fold)

    loads = [
        pltpu.make_async_copy(
            contact.at[:, pl.ds(128 * j, 128)],
            v1.at[begin + j, pl.ds(HALO, tile_rows), :],
            load_sem.at[j],
        )
        for j in range(pairs)
    ]
    weight_loads = [
        pltpu.make_async_copy(src, dst, weight_sem.at[at])
        for at, (src, dst) in enumerate(zip(weights, held))
    ]
    for load in loads + weight_loads:
        load.start()

    def clear(buf, low, high, lanes=slice(0, 128)):
        width = lanes.stop - lanes.start
        buf[low:high, :, lanes] = jnp.zeros((high - low, span, width), buf.dtype)

    def clear_rows(buf):
        strip = jnp.zeros((all_pairs, HALO, 128), buf.dtype)

        @pl.when(up_edge)
        def _():
            buf[:, 0:HALO, :] = strip

        @pl.when(down_edge)
        def _():
            buf[:, HALO + tile_rows : span, :] = strip

    def clear_outside(buf):
        clear_rows(buf)

        @pl.when(left_edge)
        def _():
            clear(buf, 0, begin)

        @pl.when(right_edge)
        def _():
            clear(buf, end, all_pairs)

    def clear_hidden(hid, s):
        clear_rows(hid)

        @pl.when(left_edge)
        def _():
            clear(hid, 0, begin, slice(0, 64))
            clear(hid, 0, begin - s, slice(64, 128))

        @pl.when(right_edge)
        def _():
            clear(hid, end, all_pairs, slice(0, 64))
            clear(hid, end - s, all_pairs, slice(64, 128))

    class Halo:
        def __init__(self, buf, send, recv):
            self.copies = {}
            for at, (dr, dc) in enumerate(ENDS + CORNERS):
                row, to_row = (HALO, HALO + tile_rows) if dr < 0 else (tile_rows, 0)
                col, cols = {-1: (0, SIDE), 0: (begin, pairs), 1: (end, SIDE)}[dc]
                self.copies[dr, dc] = pltpu.make_async_remote_copy(
                    src_ref=buf.at[pl.ds(col, cols), pl.ds(row, HALO), :],
                    dst_ref=buf.at[pl.ds(col, cols), pl.ds(to_row, HALO), :],
                    send_sem=send.at[at],
                    recv_sem=recv.at[at],
                    device_id=(jnp.clip(r + dr, 0, rows_of - 1), c),
                    device_id_type=MESH,
                )
            at = len(ENDS + CORNERS)
            for _, dc in SIDES:
                col, to_col = (begin, end) if dc < 0 else (pairs, 0)
                for part in PARTS:
                    row, rows = {
                        -1: (HALO, HALO), 0: (2 * HALO, tile_rows - 2 * HALO), 1: (tile_rows, HALO)
                    }[part]
                    self.copies[0, dc, part] = pltpu.make_async_remote_copy(
                        src_ref=buf.at[pl.ds(col, SIDE), pl.ds(row, rows), :],
                        dst_ref=buf.at[pl.ds(to_col, SIDE), pl.ds(row, rows), :],
                        send_sem=send.at[at],
                        recv_sem=recv.at[at],
                        device_id=(r, jnp.clip(c + dc, 0, cols_of - 1)),
                        device_id_type=MESH,
                    )
                    at += 1

        def start(self, dr, dc):
            pl.when(there(dr, dc))(self.copies[dr, dc].start)

        def wait_sent(self, dr, dc):
            pl.when(there(dr, dc))(self.copies[dr, dc].wait_send)

        def start_side(self, dc, part):
            pl.when(there(0, dc))(self.copies[0, dc, part].start)

        def wait_side_sent(self, dc, part):
            pl.when(there(0, dc))(self.copies[0, dc, part].wait_send)

        def wait_side(self, dc, part):
            pl.when(there(0, -dc))(self.copies[0, dc, part].wait_recv)

        def wait_end(self, dr):
            pl.when(there(-dr, 0))(self.copies[dr, 0].wait_recv)

        def wait_corner(self, dr, dc):
            pl.when(there(-dr, dc))(self.copies[dr, dc].wait_recv)

    def down(buf, hid, at, d, s, s_up, chunks):
        low, n, stride, count = chunks

        def step(i, carry):
            j = low + i * stride
            x = jnp.concatenate(
                [buf[pl.ds(j - s, n)], buf[pl.ds(j, n)], buf[pl.ds(j + s, n)]], axis=-1
            ).reshape(n * span, 384)
            sums = jnp.dot(x, wd[at], preferred_element_type=jnp.float32)
            outer, central = sums[:, :128], sums[:, 128:]
            h = pltpu.roll(outer, d, 0) + central
            h = h + pltpu.roll(pltpu.roll(outer, 64, 1), n * span - d, 0)
            h = jnp.maximum(h + bias[at : at + 1, :], 0.0)
            moved = pltpu.roll(h, 64, 1)
            hid[pl.ds(j, n), :, 0:64] = h.astype(jnp.bfloat16).reshape(n, span, 128)[:, :, 0:64]
            hid[pl.ds(j - s_up, n), :, 64:128] = moved.astype(jnp.bfloat16).reshape(n, span, 128)[
                :, :, 64:128
            ]
            return carry

        lax.fori_loop(0, count, step, 0)
        clear_hidden(hid, s_up)

    def up(hid, at, d, s, chunks, store):
        low, n, stride, count = chunks

        def step(i, carry):
            j = low + i * stride
            x = jnp.concatenate([hid[pl.ds(j - s, n)], hid[pl.ds(j + s, n)]], axis=-1)
            sums = jnp.dot(x.reshape(n * span, 256), wu[at], preferred_element_type=jnp.float32)
            u = pltpu.roll(sums[:, :128], d, 0) + sums[:, 128:256]
            u = u + pltpu.roll(sums[:, 256:], n * span - d, 0)
            u = (u + bias[4 + at : 5 + at, :]).reshape(n, span, 128)
            store(j, n, u)
            return carry

        lax.fori_loop(0, count, step, 0)

    def section(buf, halo, at, store_last):
        (d1, d2), (d3, d4) = BLOCKS
        s1, s2, s3, s4 = max(d1 // 2, 1), d2 // 2, d3 // 2, d4 // 2

        def store(j, n, u):
            v = buf[pl.ds(j, n)].astype(jnp.float32) + u
            middle[pl.ds(j, n)] = v.astype(jnp.bfloat16)

        def one(chunks):
            down(buf, hid1, at, d1, s1, s2, chunks)

        def two(chunks):
            up(hid1, at, d2, s2, chunks, store)
            clear_outside(middle)

        def three(chunks):
            down(middle, hid2, at + 1, d3, s3, s4, chunks)

        def centre(t):
            n = chunk_of(pairs - 2 * t, 8)
            return begin + t, n, n, (pairs - 2 * t) // n

        def side_chunk(t, i):
            return t + i * (end - 2 * t), SIDE, 0, 1

        t1, t2, t3 = s1, s1 + s2, s1 + s2 + s3
        for dr in (-1, 1):
            halo.wait_end(dr)
        one(centre(t1))
        for dc in (-1, 1):
            for dr in (-1, 1):
                halo.wait_side(-dc, dr)
                halo.start(dr, dc)
        two(centre(t2))
        three(centre(t3))

        def side(i, carry):
            for k, (_, dc) in enumerate(SIDES):

                @pl.when(i == k)
                def _():
                    halo.wait_side(-dc, 0)
                    for dr in (-1, 1):
                        halo.wait_corner(dr, dc)

            one(side_chunk(t1, i))
            two(side_chunk(t2, i))
            three(side_chunk(t3, i))
            return carry

        lax.fori_loop(0, 2, side, 0)
        up(hid2, at + 1, d4, s4, centre(0), store_last)
        for way in ENDS + CORNERS:
            halo.wait_sent(*way)
        for _, dc in SIDES:
            for part in PARTS:
                halo.wait_side_sent(dc, part)

    for load in loads:
        load.wait()
    pl.semaphore_wait(barrier, greeted)
    halo1 = Halo(v1, send1, recv1)
    halo2 = Halo(v2, send2, recv2)
    for way in ENDS:
        halo1.start(*way)
    for part in PARTS:
        for _, dc in SIDES:
            halo1.start_side(dc, part)

    clear_outside(v1)
    clear_outside(v2)
    for ref in (hid1, hid2, wu, bias):
        ref[...] = jnp.zeros(ref.shape, ref.dtype)
    for load in weight_loads:
        load.wait()
    for sec, (dw, db, uw, ub) in enumerate(((fd, fdb, fu, fub), (sd, sdb, su, sub))):
        for block, (d1, d2) in enumerate(BLOCKS):
            at = 2 * sec + block
            wide_down[...] = jnp.zeros(wide_down.shape, wide_down.dtype)
            bias[at : at + 1, 0:32] = db[block : block + 1, :]
            bias[at : at + 1, 32:64] = db[block : block + 1, :]
            bias[4 + at : 5 + at, 0:64] = ub[block : block + 1, :]
            bias[4 + at : 5 + at, 64:128] = ub[block : block + 1, :]
            for p in range(3):
                group = (0, 128, 64)[p]
                for q in range(3):
                    for par in range(2):
                        shift = par + (q - 1) * d1
                        third = 1 + (shift // 2 > 0) - (shift // 2 < 0)
                        lane = third * 128 + (shift % 2) * 64
                        row = group + par * 32
                        wide_down[row : row + 32, lane : lane + 64] = dw[block, p, q]
                        row = q * 64 + par * 32
                        lane = p * 128 + par * 64
                        wu[at, row : row + 32, lane : lane + 64] = uw[block, p, q]
            wd[at] = wide_down[...].T

    def store_first(j, n, u):
        v = middle[pl.ds(j, n), inner, :].astype(jnp.float32) + u[:, inner, :]
        first[pl.ds(j - begin, n)] = v.astype(jnp.bfloat16)

    section(v1, halo1, 0, store_first)

    def piece(half, m):
        return first.at[:, pl.ds(m * square + half * half_rows, half_rows), :]

    for m in range(fold):

        @pl.when(away)
        def _():
            pltpu.make_async_remote_copy(
                src_ref=piece(1, m),
                dst_ref=passing.at[mine, m],
                send_sem=send_m.at[m, 1],
                recv_sem=pass_recv.at[mine, m],
                device_id=relay,
                device_id_type=MESH,
            ).start()

    mirrors = {}
    for half in range(2):
        for m, peer in enumerate(peers):
            remote = pltpu.make_async_remote_copy(
                src_ref=piece(half, m),
                dst_ref=mirror.at[slot, half],
                send_sem=send_m.at[m, half],
                recv_sem=recv_m.at[slot, half],
                device_id=peer,
                device_id_type=MESH,
            )
            here = pltpu.make_async_copy(piece(half, m), mirror.at[slot, half], local_sem.at[half])
            direct = jnp.logical_not(is_me(peer))
            if half == 1:
                direct = direct & home
            pl.when(direct)(remote.start)
            pl.when(is_me(peer))(here.start)
            mirrors[half, m] = (peer, remote, here)

    def passed(i, m):
        return pltpu.make_async_remote_copy(
            src_ref=passing.at[i, m],
            dst_ref=mirror.at[slot, 1],
            send_sem=pass_send.at[i, m],
            recv_sem=recv_m.at[slot, 1],
            device_id=(mirror_row, fold * (2 * i + parity) + m),
            device_id_type=MESH,
        )

    for i in range(rows_of // 2):

        @pl.when(home & (mine != i))
        def _():
            for m in range(fold):
                pltpu.make_async_remote_copy(
                    src_ref=passing.at[i, m],
                    dst_ref=passing.at[i, m],
                    send_sem=pass_send.at[i, m],
                    recv_sem=pass_recv.at[i, m],
                    device_id=(2 * i + parity, c),
                    device_id_type=MESH,
                ).wait_recv()
                passed(i, m).start()

    low_half = lax.broadcasted_iota(jnp.int32, (pairs, 128), 1) < 64
    for half in range(2):
        for m in range(fold):
            peer, remote, here = mirrors[half, m]
            arrived = pltpu.make_async_remote_copy(
                src_ref=mirror.at[m, half],
                dst_ref=mirror.at[m, half],
                send_sem=send_m.at[m, half],
                recv_sem=recv_m.at[m, half],
                device_id=peer,
                device_id_type=MESH,
            )
            pl.when(jnp.logical_not(is_me(peer)))(arrived.wait_recv)
            pl.when(is_me(peer))(here.wait)
        for m in range(fold):
            at = half * fold + m
            wide[at] = mirror[m, half].astype(jnp.float32).reshape(pairs * half_rows, 128)
            for j in range(half_pairs):
                even = wide[at, pl.ds(2 * j, pairs, stride=half_rows), :]
                odd = wide[at, pl.ds(2 * j + 1, pairs, stride=half_rows), :]
                base = (half * half_pairs + j) * tile_rows + m * square
                flipped[pl.ds(base, pairs, stride=2), :] = jnp.where(
                    low_half, even, pltpu.roll(odd, 64, 1)
                )
                flipped[pl.ds(base + 1, pairs, stride=2), :] = jnp.where(
                    low_half, pltpu.roll(even, 64, 1), odd
                )
        low = half * half_pairs
        own = first[low : low + half_pairs].astype(jnp.float32)
        turned = flipped[low * tile_rows : (low + half_pairs) * tile_rows, :]
        both = (own + turned.reshape(half_pairs, tile_rows, 128)) * 0.5
        v2[begin + low : begin + low + half_pairs, inner, :] = both.astype(jnp.bfloat16)
        for part in PARTS:
            halo2.start_side(2 * half - 1, part)
    for way in ENDS:
        halo2.start(*way)
    for half in range(2):
        for m in range(fold):
            peer, remote, here = mirrors[half, m]
            pl.when(jnp.logical_not(is_me(peer)))(remote.wait_send)
    for i in range(rows_of // 2):

        @pl.when(home & (mine != i))
        def _():
            for m in range(fold):
                passed(i, m).wait_send()

    def store_second(j, n, u):
        v = (middle[pl.ds(j, n), inner, :].astype(jnp.float32) + u[:, inner, :]).astype(jnp.bfloat16)
        for k in range(n):
            out[:, pl.ds(pl.multiple_of((j - begin + k) * 128, 128), 128)] = v[k]

    section(v2, halo2, 2, store_second)


def per_device(rows_of, cols_of, contact, *weights):
    tile_rows = contact.shape[0]
    pairs = contact.shape[1] // 128
    span, all_pairs, square = tile_rows + 2 * HALO, pairs + 2 * SIDE, 2 * pairs
    fold = tile_rows // square
    weights = [w.swapaxes(3, 4) if at in (2, 6) else w for at, w in enumerate(weights)]
    ways = len(SIDES) * len(PARTS) + len(ENDS + CORNERS)
    buf = pltpu.VMEM((all_pairs, span, 128), jnp.bfloat16)
    return pl.pallas_call(
        functools.partial(kernel, rows_of, cols_of),
        out_shape=jax.ShapeDtypeStruct(contact.shape, jnp.bfloat16),
        in_specs=[pl.BlockSpec(memory_space=pl.ANY)] * (1 + len(weights)),
        out_specs=pl.BlockSpec(memory_space=pltpu.VMEM),
        scratch_shapes=[
            *(pltpu.VMEM(w.shape, w.dtype) for w in weights),
            buf,
            buf,
            buf,
            buf,
            buf,
            pltpu.VMEM((pairs, tile_rows, 128), jnp.bfloat16),
            pltpu.VMEM((fold, 2, pairs, pairs, 128), jnp.bfloat16),
            pltpu.VMEM((rows_of // 2, fold, pairs, pairs, 128), jnp.bfloat16),
            pltpu.VMEM((2 * fold, pairs * pairs, 128), jnp.float32),
            pltpu.VMEM((pairs * tile_rows, 128), jnp.float32),
            pltpu.VMEM((256, 384), jnp.bfloat16),
            pltpu.VMEM((4, 384, 256), jnp.bfloat16),
            pltpu.VMEM((4, 256, 384), jnp.bfloat16),
            pltpu.VMEM((8, 128), jnp.float32),
            pltpu.SemaphoreType.DMA((ways,)),
            pltpu.SemaphoreType.DMA((ways,)),
            pltpu.SemaphoreType.DMA((ways,)),
            pltpu.SemaphoreType.DMA((ways,)),
            pltpu.SemaphoreType.DMA((fold, 2)),
            pltpu.SemaphoreType.DMA((fold, 2)),
            pltpu.SemaphoreType.DMA((rows_of // 2, fold)),
            pltpu.SemaphoreType.DMA((rows_of // 2, fold)),
            pltpu.SemaphoreType.DMA((2,)),
            pltpu.SemaphoreType.DMA((pairs,)),
            pltpu.SemaphoreType.DMA((len(weights),)),
        ],
        compiler_params=pltpu.CompilerParams(
            collective_id=0, has_side_effects=True, vmem_limit_bytes=56 * 1024 * 1024
        ),
    )(contact, *weights)


def solution(mesh):
    in_specs = (P("row", "col"), P(), P(), P(), P(), P(), P(), P(), P())
    return jax.shard_map(
        functools.partial(per_device, mesh.shape["row"], mesh.shape["col"]),
        mesh=mesh,
        in_specs=in_specs,
        out_specs=P("row", "col"),
        check_vma=False,
    )
```

```python
import functools

import jax
import jax.numpy as jnp
from jax import lax
from jax.experimental import pallas as pl
from jax.experimental.pallas import tpu as pltpu
from jax.sharding import PartitionSpec as P

MESH = pl.DeviceIdType.MESH
HALO = 16
SIDE = HALO // 2
BLOCKS = ((1, 2), (4, 8))
SIDES = ((0, -1), (0, 1))
PARTS = (-1, 1, 0)
ENDS = ((-1, 0), (1, 0))
CORNERS = ((-1, -1), (-1, 1), (1, -1), (1, 1))


def chunk_of(count, most):
    return max(n for n in range(1, most + 1) if count % n == 0)


def kernel(
    rows_of, cols_of,
    contact, *refs,
):
    weights, (out,), held = refs[:8], refs[8:9], refs[9:17]
    (
    v1, v2, middle, hid1, hid2, first, mirror, passing, wide, flipped, wide_down, wd, wu, bias,
    send1, recv1, send2, recv2, send_m, recv_m, pass_recv, pass_send, local_sem, load_sem, weight_sem,
    ) = refs[17:]
    fd, fdb, fu, fub, sd, sdb, su, sub = held
    tile_rows = contact.shape[0]
    pairs = contact.shape[1] // 128
    span = tile_rows + 2 * HALO
    all_pairs = pairs + 2 * SIDE
    square = 2 * pairs
    fold = tile_rows // square
    half_rows, half_pairs = square // 2, pairs // 2
    begin, end = SIDE, SIDE + pairs
    inner = slice(HALO, HALO + tile_rows)
    r = lax.axis_index("row")
    c = lax.axis_index("col")
    up_edge, down_edge = r == 0, r == rows_of - 1
    left_edge, right_edge = c == 0, c == cols_of - 1

    def there(dr, dc):
        return (r + dr >= 0) & (r + dr < rows_of) & (c + dc >= 0) & (c + dc < cols_of)

    mirror_row = lax.div(c, fold)
    peers = [(mirror_row, fold * r + m) for m in range(fold)]
    slot = lax.rem(c, fold)

    def is_me(peer):
        return (peer[0] == r) & (peer[1] == c)

    loads = [
        pltpu.make_async_copy(
            contact.at[:, pl.ds(128 * j, 128)],
            v1.at[begin + j, pl.ds(HALO, tile_rows), :],
            load_sem.at[j],
        )
        for j in range(pairs)
    ]
    weight_loads = [
        pltpu.make_async_copy(src, dst, weight_sem.at[at])
        for at, (src, dst) in enumerate(zip(weights, held))
    ]
    for load in loads + weight_loads:
        load.start()

    barrier = pltpu.get_barrier_semaphore()
    greeted = jnp.int32(0)
    for dr, dc in SIDES + ENDS:
        ok = there(dr, dc)
        greeted += ok.astype(jnp.int32)

        @pl.when(ok)
        def _():
            pl.semaphore_signal(barrier, inc=1, device_id=(r + dr, c + dc), device_id_type=MESH)

    for peer in peers:
        other = jnp.logical_not(is_me(peer))
        greeted += other.astype(jnp.int32)

        @pl.when(other)
        def _():
            pl.semaphore_signal(barrier, inc=1, device_id=peer, device_id_type=MESH)

    mine, parity = lax.div(r, 2), lax.rem(r, 2)
    home = lax.div(mirror_row, 2) == mine
    away = jnp.logical_not(home)
    relay = (2 * lax.div(mirror_row, 2) + parity, c)

    @pl.when(away)
    def _():
        pl.semaphore_signal(barrier, inc=1, device_id=relay, device_id_type=MESH)
        for m in range(fold):
            giver = (2 * mine + lax.rem(mirror_row, 2), fold * r + m)
            pl.semaphore_signal(barrier, inc=1, device_id=giver, device_id_type=MESH)

    for i in range(rows_of // 2):

        @pl.when(home & (mine != i))
        def _():
            served = 2 * i + parity
            for partner in [(served, c)] + [(mirror_row, fold * served + m) for m in range(fold)]:
                pl.semaphore_signal(barrier, inc=1, device_id=partner, device_id_type=MESH)

    greeted += jnp.where(home, (rows_of // 2 - 1) * (1 + fold), 1 + fold)

    def clear(buf, low, high, lanes=slice(0, 128)):
        width = lanes.stop - lanes.start
        buf[low:high, :, lanes] = jnp.zeros((high - low, span, width), buf.dtype)

    def clear_rows(buf):
        strip = jnp.zeros((all_pairs, HALO, 128), buf.dtype)

        @pl.when(up_edge)
        def _():
            buf[:, 0:HALO, :] = strip

        @pl.when(down_edge)
        def _():
            buf[:, HALO + tile_rows : span, :] = strip

    def clear_outside(buf):
        clear_rows(buf)

        @pl.when(left_edge)
        def _():
            clear(buf, 0, begin)

        @pl.when(right_edge)
        def _():
            clear(buf, end, all_pairs)

    def clear_hidden(hid, s):
        clear_rows(hid)

        @pl.when(left_edge)
        def _():
            clear(hid, 0, begin, slice(0, 64))
            clear(hid, 0, begin - s, slice(64, 128))

        @pl.when(right_edge)
        def _():
            clear(hid, end, all_pairs, slice(0, 64))
            clear(hid, end - s, all_pairs, slice(64, 128))

    class Halo:
        def __init__(self, buf, send, recv):
            self.copies = {}
            for at, (dr, dc) in enumerate(ENDS + CORNERS):
                row, to_row = (HALO, HALO + tile_rows) if dr < 0 else (tile_rows, 0)
                col, cols = {-1: (0, SIDE), 0: (begin, pairs), 1: (end, SIDE)}[dc]
                self.copies[dr, dc] = pltpu.make_async_remote_copy(
                    src_ref=buf.at[pl.ds(col, cols), pl.ds(row, HALO), :],
                    dst_ref=buf.at[pl.ds(col, cols), pl.ds(to_row, HALO), :],
                    send_sem=send.at[at],
                    recv_sem=recv.at[at],
                    device_id=(jnp.clip(r + dr, 0, rows_of - 1), c),
                    device_id_type=MESH,
                )
            at = len(ENDS + CORNERS)
            for _, dc in SIDES:
                col, to_col = (begin, end) if dc < 0 else (pairs, 0)
                for part in PARTS:
                    row, rows = {
                        -1: (HALO, HALO), 0: (2 * HALO, tile_rows - 2 * HALO), 1: (tile_rows, HALO)
                    }[part]
                    self.copies[0, dc, part] = pltpu.make_async_remote_copy(
                        src_ref=buf.at[pl.ds(col, SIDE), pl.ds(row, rows), :],
                        dst_ref=buf.at[pl.ds(to_col, SIDE), pl.ds(row, rows), :],
                        send_sem=send.at[at],
                        recv_sem=recv.at[at],
                        device_id=(r, jnp.clip(c + dc, 0, cols_of - 1)),
                        device_id_type=MESH,
                    )
                    at += 1

        def start(self, dr, dc):
            pl.when(there(dr, dc))(self.copies[dr, dc].start)

        def wait_sent(self, dr, dc):
            pl.when(there(dr, dc))(self.copies[dr, dc].wait_send)

        def start_side(self, dc, part):
            pl.when(there(0, dc))(self.copies[0, dc, part].start)

        def wait_side_sent(self, dc, part):
            pl.when(there(0, dc))(self.copies[0, dc, part].wait_send)

        def wait_side(self, dc, part):
            pl.when(there(0, -dc))(self.copies[0, dc, part].wait_recv)

        def wait_end(self, dr):
            pl.when(there(-dr, 0))(self.copies[dr, 0].wait_recv)

        def wait_corner(self, dr, dc):
            pl.when(there(-dr, dc))(self.copies[dr, dc].wait_recv)

    def down(buf, hid, at, d, s, s_up, chunks):
        low, n, stride, count = chunks

        def step(i, carry):
            j = low + i * stride
            x = jnp.concatenate(
                [buf[pl.ds(j - s, n)], buf[pl.ds(j, n)], buf[pl.ds(j + s, n)]], axis=-1
            ).reshape(n * span, 384)
            sums = jnp.dot(x, wd[at], preferred_element_type=jnp.float32)
            outer, central = sums[:, :128], sums[:, 128:]
            h = pltpu.roll(outer, d, 0) + central
            h = h + pltpu.roll(pltpu.roll(outer, 64, 1), n * span - d, 0)
            h = jnp.maximum(h + bias[at : at + 1, :], 0.0)
            moved = pltpu.roll(h, 64, 1)
            hid[pl.ds(j, n), :, 0:64] = h.astype(jnp.bfloat16).reshape(n, span, 128)[:, :, 0:64]
            hid[pl.ds(j - s_up, n), :, 64:128] = moved.astype(jnp.bfloat16).reshape(n, span, 128)[
                :, :, 64:128
            ]
            return carry

        lax.fori_loop(0, count, step, 0)
        clear_hidden(hid, s_up)

    def up(hid, at, d, s, chunks, store):
        low, n, stride, count = chunks

        def step(i, carry):
            j = low + i * stride
            x = jnp.concatenate([hid[pl.ds(j - s, n)], hid[pl.ds(j + s, n)]], axis=-1)
            sums = jnp.dot(x.reshape(n * span, 256), wu[at], preferred_element_type=jnp.float32)
            u = pltpu.roll(sums[:, :128], d, 0) + sums[:, 128:256]
            u = u + pltpu.roll(sums[:, 256:], n * span - d, 0)
            u = (u + bias[4 + at : 5 + at, :]).reshape(n, span, 128)
            store(j, n, u)
            return carry

        lax.fori_loop(0, count, step, 0)

    def section(buf, halo, at, store_last):
        (d1, d2), (d3, d4) = BLOCKS
        s1, s2, s3, s4 = max(d1 // 2, 1), d2 // 2, d3 // 2, d4 // 2

        def store(j, n, u):
            v = buf[pl.ds(j, n)].astype(jnp.float32) + u
            middle[pl.ds(j, n)] = v.astype(jnp.bfloat16)

        def one(chunks):
            down(buf, hid1, at, d1, s1, s2, chunks)

        def two(chunks):
            up(hid1, at, d2, s2, chunks, store)
            clear_outside(middle)

        def three(chunks):
            down(middle, hid2, at + 1, d3, s3, s4, chunks)

        def centre(t):
            n = chunk_of(pairs - 2 * t, 8)
            return begin + t, n, n, (pairs - 2 * t) // n

        def sides(t):
            return t, SIDE, end - 2 * t, 2

        t1, t2, t3 = s1, s1 + s2, s1 + s2 + s3
        for dr in (-1, 1):
            halo.wait_end(dr)
        one(centre(t1))
        for dc in (-1, 1):
            for dr in (-1, 1):
                halo.wait_side(-dc, dr)
                halo.start(dr, dc)
        two(centre(t2))
        three(centre(t3))
        for dc in (-1, 1):
            halo.wait_side(dc, 0)
        for dr, dc in CORNERS:
            halo.wait_corner(dr, dc)
        one(sides(t1))
        two(sides(t2))
        three(sides(t3))
        up(hid2, at + 1, d4, s4, centre(0), store_last)
        for way in ENDS + CORNERS:
            halo.wait_sent(*way)
        for _, dc in SIDES:
            for part in PARTS:
                halo.wait_side_sent(dc, part)

    for load in loads:
        load.wait()
    pl.semaphore_wait(barrier, greeted)
    halo1 = Halo(v1, send1, recv1)
    halo2 = Halo(v2, send2, recv2)
    for way in ENDS:
        halo1.start(*way)
    for part in PARTS:
        for _, dc in SIDES:
            halo1.start_side(dc, part)

    clear_outside(v1)
    clear_outside(v2)
    for ref in (hid1, hid2, wu, bias):
        ref[...] = jnp.zeros(ref.shape, ref.dtype)
    for load in weight_loads:
        load.wait()
    def build(sec, dw, db, uw, ub):
        for block, (d1, d2) in enumerate(BLOCKS):
            at = 2 * sec + block
            wide_down[...] = jnp.zeros(wide_down.shape, wide_down.dtype)
            bias[at : at + 1, 0:32] = db[block : block + 1, :]
            bias[at : at + 1, 32:64] = db[block : block + 1, :]
            bias[4 + at : 5 + at, 0:64] = ub[block : block + 1, :]
            bias[4 + at : 5 + at, 64:128] = ub[block : block + 1, :]
            for p in range(3):
                group = (0, 128, 64)[p]
                for q in range(3):
                    for par in range(2):
                        shift = par + (q - 1) * d1
                        third = 1 + (shift // 2 > 0) - (shift // 2 < 0)
                        lane = third * 128 + (shift % 2) * 64
                        row = group + par * 32
                        wide_down[row : row + 32, lane : lane + 64] = dw[block, p, q]
                        row = q * 64 + par * 32
                        lane = p * 128 + par * 64
                        wu[at, row : row + 32, lane : lane + 64] = uw[block, p, q]
            wd[at] = wide_down[...].T

    build(0, fd, fdb, fu, fub)

    def store_first(j, n, u):
        v = middle[pl.ds(j, n), inner, :].astype(jnp.float32) + u[:, inner, :]
        first[pl.ds(j - begin, n)] = v.astype(jnp.bfloat16)

    section(v1, halo1, 0, store_first)

    def piece(half, m):
        return first.at[:, pl.ds(m * square + half * half_rows, half_rows), :]

    for m in range(fold):

        @pl.when(away)
        def _():
            pltpu.make_async_remote_copy(
                src_ref=piece(1, m),
                dst_ref=passing.at[mine, m],
                send_sem=send_m.at[m, 1],
                recv_sem=pass_recv.at[mine, m],
                device_id=relay,
                device_id_type=MESH,
            ).start()

    mirrors = {}
    for half in range(2):
        for m, peer in enumerate(peers):
            remote = pltpu.make_async_remote_copy(
                src_ref=piece(half, m),
                dst_ref=mirror.at[slot, half],
                send_sem=send_m.at[m, half],
                recv_sem=recv_m.at[slot, half],
                device_id=peer,
                device_id_type=MESH,
            )
            here = pltpu.make_async_copy(piece(half, m), mirror.at[slot, half], local_sem.at[half])
            direct = jnp.logical_not(is_me(peer))
            if half == 1:
                direct = direct & home
            pl.when(direct)(remote.start)
            pl.when(is_me(peer))(here.start)
            mirrors[half, m] = (peer, remote, here)

    build(1, sd, sdb, su, sub)

    def passed(i, m):
        return pltpu.make_async_remote_copy(
            src_ref=passing.at[i, m],
            dst_ref=mirror.at[slot, 1],
            send_sem=pass_send.at[i, m],
            recv_sem=recv_m.at[slot, 1],
            device_id=(mirror_row, fold * (2 * i + parity) + m),
            device_id_type=MESH,
        )

    for i in range(rows_of // 2):

        @pl.when(home & (mine != i))
        def _():
            for m in range(fold):
                pltpu.make_async_remote_copy(
                    src_ref=passing.at[i, m],
                    dst_ref=passing.at[i, m],
                    send_sem=pass_send.at[i, m],
                    recv_sem=pass_recv.at[i, m],
                    device_id=(2 * i + parity, c),
                    device_id_type=MESH,
                ).wait_recv()
                passed(i, m).start()

    low_half = lax.broadcasted_iota(jnp.int32, (pairs, 128), 1) < 64
    for half in range(2):
        for m in range(fold):
            peer, remote, here = mirrors[half, m]
            arrived = pltpu.make_async_remote_copy(
                src_ref=mirror.at[m, half],
                dst_ref=mirror.at[m, half],
                send_sem=send_m.at[m, half],
                recv_sem=recv_m.at[m, half],
                device_id=peer,
                device_id_type=MESH,
            )
            pl.when(jnp.logical_not(is_me(peer)))(arrived.wait_recv)
            pl.when(is_me(peer))(here.wait)
        for m in range(fold):
            at = half * fold + m
            wide[at] = mirror[m, half].astype(jnp.float32).reshape(pairs * half_rows, 128)
            for j in range(half_pairs):
                even = wide[at, pl.ds(2 * j, pairs, stride=half_rows), :]
                odd = wide[at, pl.ds(2 * j + 1, pairs, stride=half_rows), :]
                base = (half * half_pairs + j) * tile_rows + m * square
                flipped[pl.ds(base, pairs, stride=2), :] = jnp.where(
                    low_half, even, pltpu.roll(odd, 64, 1)
                )
                flipped[pl.ds(base + 1, pairs, stride=2), :] = jnp.where(
                    low_half, pltpu.roll(even, 64, 1), odd
                )
        low = half * half_pairs
        own = first[low : low + half_pairs].astype(jnp.float32)
        turned = flipped[low * tile_rows : (low + half_pairs) * tile_rows, :]
        both = (own + turned.reshape(half_pairs, tile_rows, 128)) * 0.5
        v2[begin + low : begin + low + half_pairs, inner, :] = both.astype(jnp.bfloat16)
        for part in PARTS:
            halo2.start_side(2 * half - 1, part)
    for way in ENDS:
        halo2.start(*way)
    for half in range(2):
        for m in range(fold):
            peer, remote, here = mirrors[half, m]
            pl.when(jnp.logical_not(is_me(peer)))(remote.wait_send)
    for i in range(rows_of // 2):

        @pl.when(home & (mine != i))
        def _():
            for m in range(fold):
                passed(i, m).wait_send()

    def store_second(j, n, u):
        v = (middle[pl.ds(j, n), inner, :].astype(jnp.float32) + u[:, inner, :]).astype(jnp.bfloat16)
        for k in range(n):
            out[:, pl.ds(pl.multiple_of((j - begin + k) * 128, 128), 128)] = v[k]

    section(v2, halo2, 2, store_second)


def per_device(rows_of, cols_of, contact, *weights):
    tile_rows = contact.shape[0]
    pairs = contact.shape[1] // 128
    span, all_pairs, square = tile_rows + 2 * HALO, pairs + 2 * SIDE, 2 * pairs
    fold = tile_rows // square
    weights = [w.swapaxes(3, 4) if at in (2, 6) else w for at, w in enumerate(weights)]
    ways = len(SIDES) * len(PARTS) + len(ENDS + CORNERS)
    buf = pltpu.VMEM((all_pairs, span, 128), jnp.bfloat16)
    return pl.pallas_call(
        functools.partial(kernel, rows_of, cols_of),
        out_shape=jax.ShapeDtypeStruct(contact.shape, jnp.bfloat16),
        in_specs=[pl.BlockSpec(memory_space=pl.ANY)] * (1 + len(weights)),
        out_specs=pl.BlockSpec(memory_space=pltpu.VMEM),
        scratch_shapes=[
            *(pltpu.VMEM(w.shape, w.dtype) for w in weights),
            buf,
            buf,
            buf,
            buf,
            buf,
            pltpu.VMEM((pairs, tile_rows, 128), jnp.bfloat16),
            pltpu.VMEM((fold, 2, pairs, pairs, 128), jnp.bfloat16),
            pltpu.VMEM((rows_of // 2, fold, pairs, pairs, 128), jnp.bfloat16),
            pltpu.VMEM((2 * fold, pairs * pairs, 128), jnp.float32),
            pltpu.VMEM((pairs * tile_rows, 128), jnp.float32),
            pltpu.VMEM((256, 384), jnp.bfloat16),
            pltpu.VMEM((4, 384, 256), jnp.bfloat16),
            pltpu.VMEM((4, 256, 384), jnp.bfloat16),
            pltpu.VMEM((8, 128), jnp.float32),
            pltpu.SemaphoreType.DMA((ways,)),
            pltpu.SemaphoreType.DMA((ways,)),
            pltpu.SemaphoreType.DMA((ways,)),
            pltpu.SemaphoreType.DMA((ways,)),
            pltpu.SemaphoreType.DMA((fold, 2)),
            pltpu.SemaphoreType.DMA((fold, 2)),
            pltpu.SemaphoreType.DMA((rows_of // 2, fold)),
            pltpu.SemaphoreType.DMA((rows_of // 2, fold)),
            pltpu.SemaphoreType.DMA((2,)),
            pltpu.SemaphoreType.DMA((pairs,)),
            pltpu.SemaphoreType.DMA((len(weights),)),
        ],
        compiler_params=pltpu.CompilerParams(
            collective_id=0, has_side_effects=True, vmem_limit_bytes=56 * 1024 * 1024
        ),
    )(contact, *weights)


def solution(mesh):
    in_specs = (P("row", "col"), P(), P(), P(), P(), P(), P(), P(), P())
    return jax.shard_map(
        functools.partial(per_device, mesh.shape["row"], mesh.shape["col"]),
        mesh=mesh,
        in_specs=in_specs,
        out_specs=P("row", "col"),
        check_vma=False,
    )
```
